256 devices in a mesh: lat: 16 (over x, y_hi, core), lon: 16 (over y_lo, z).
Axes of the slice: x: 4, y: 4 (y_hi: 2, y_lo: 2; y = y_hi * 2 + y_lo), z: 8, core: 2. Of those that a mesh axis runs over, the one named last changes fastest.
Arguments:
- tracer: float32 [32, 512, 2048], P(None, 'lat', 'lon'), may hold values from -6 to 6
- source: int32 [512, 16], P('lat', 'lon'), may hold values from 0 to 8191, as said below
- offset: int32 [512, 2048], P('lat', 'lon'), may hold values from 1 to 125
- fraction: float32 [512, 2048], P('lat', 'lon'), may hold values from 0 to 1
- cutoffs: int32 [2, 8], replicated, may hold values from 2 to 255
Outputs:
- advected: float32 [32, 512, 2048], P(None, 'lat', 'lon')
The draws below stay inside these ranges and needn't reach their ends.
Inputs may be any that keep to these rules, and one draw needn't show every extreme that they name: With source[j, b] = rho * 16 + beta: |rho - j| <= 2, and some arrival blocks reach 2 in both directions. Rows j with 8 <= j < 504 have beta equal to b - 1, b or b + 1 modulo 16. Rows within 8 of a pole have rho within the same band of 8 rows at that pole and beta anywhere on the circle.
All inputs are finite; a program needn't handle non-finite values.
Results may differ from the reference program's by a relative error of at most 0.000071.
Values sent between devices are 32-bit elements; how exact they have to be, the bound alone decides.
No kernel may reach another device: no remote copies, remote signals or barrier semaphores. Data moves between devices by JAX's collectives and lax.ppermute only.
A program may use at most 128 MiB of HBM per device.

```python
import jax
import jax.numpy as jnp
from jax import lax

NLON = 2048
BLK = 128
HL = 2
PROWS = 8
C = 32
NLAT = 512
NBLK = 16


def draw_source(key, part):
    row_key, step_key = jax.random.split(jax.random.fold_in(key, 17), 2)
    row_ids = jnp.arange(NLAT, dtype=jnp.int32)[:, None]
    blocks = jnp.arange(NBLK, dtype=jnp.int32)[None, :]
    row_step = jax.random.randint(row_key, (NLAT, NBLK), -HL, HL + 1)
    serial = row_ids * NBLK + blocks
    row_step = jnp.where(serial % 97 == 5, HL, row_step)
    row_step = jnp.where(serial % 97 == 11, -HL, row_step)
    pole_distance = jnp.minimum(row_ids, NLAT - 1 - row_ids)
    near_pole = pole_distance < PROWS
    northern = row_ids < NLAT // 2
    lowest_row = jnp.where(near_pole & jnp.logical_not(northern), NLAT - PROWS, 0)
    highest_row = jnp.where(near_pole & northern, PROWS - 1, NLAT - 1)
    start_row = jnp.clip(row_ids + row_step, lowest_row, highest_row)
    block_reach = jnp.where(near_pole, 1 + (NBLK // 2 - 1) * (PROWS - pole_distance) // PROWS, 1)
    random_bits = jax.random.randint(step_key, (NLAT, NBLK), 0, 1 << 20)
    block_shift = random_bits % (2 * block_reach + 1) - block_reach
    start_block = jnp.mod(blocks + block_shift, NBLK)
    return (start_row * NBLK + start_block).astype(jnp.int32)


def with_ends(values, stream_key, least, top_value):
    dims = values.shape
    spot = [jax.random.randint(jax.random.fold_in(stream_key, axis), (), 0, dims[axis]) for axis in range(len(dims))]
    values = values.at[tuple(spot)].set(least)
    longest = dims.index(max(dims))
    spot[longest] = (spot[longest] + 1) % dims[longest]
    return values.at[tuple(spot)].set(top_value)


def levels(stream_key, dims, cuts, low, top_value):
    factor_of, own = 1.0, jax.random.fold_in(stream_key, 6)
    for axis_at, blocks in cuts:
        heights = jnp.exp(jax.random.uniform(jax.random.fold_in(own, axis_at), (blocks,), jnp.float32, low / len(cuts), top_value / len(cuts)))
        factor_of = factor_of * jnp.repeat(heights, dims[axis_at] // blocks).reshape([-1 if axis == axis_at else 1 for axis in range(len(dims))])
    return factor_of


def scatter_about(rng, shape, deviation, limit, cuts=(), kind=jnp.bfloat16):
    drawn = deviation * jax.random.normal(rng, shape, jnp.float32)
    if cuts:
        drawn = drawn * levels(rng, shape, cuts, -0.22, 0.18)
    return jnp.clip(drawn, -limit, limit).astype(kind)


def setup_inputs(seed: int = 0) -> dict:
    keys = jax.random.split(jax.random.key(seed), 6)
    return {
        "tracer": scatter_about(keys[0], (C, NLAT, NLON), 1.0, 6.0, ((1, 16), (2, 16)), jnp.float32),
        "source": draw_source(jax.random.fold_in(keys[5], 71), 0),
        "offset": with_ends(jax.random.randint(keys[2], (NLAT, NLON), 1, BLK - 2), jax.random.fold_in(keys[2], 1), 1, (BLK - 2) - 1).astype(jnp.int32),
        "fraction": jnp.clip(1.0 * jax.random.uniform(keys[3], (NLAT, NLON), jnp.float32) ** levels(keys[3], (NLAT, NLON), ((0, 16), (1, 16)), -0.2, 0.2), 0.0, 1.0),
        "cutoffs": with_ends(jax.random.randint(keys[4], (2, PROWS), 2, NLON // 8), jax.random.fold_in(keys[4], 1), 2, (NLON // 8) - 1).astype(jnp.int32),
    }


def cubic_limited(before_one, at_anchor, after_one, after_two, position):
    weight_before = -position * (position - 1.0) * (position - 2.0) / 6.0
    weight_anchor = (position + 1.0) * (position - 1.0) * (position - 2.0) / 2.0
    weight_after = -(position + 1.0) * position * (position - 2.0) / 2.0
    weight_beyond = (position + 1.0) * position * (position - 1.0) / 6.0
    interpolated = weight_before * before_one + weight_anchor * at_anchor + weight_after * after_one + weight_beyond * after_two
    lowest_bound = jnp.minimum(at_anchor, after_one)
    upper_bound = jnp.maximum(at_anchor, after_one)
    return jnp.minimum(jnp.maximum(interpolated, lowest_bound), upper_bound)


def reference(tracer, source, offset, fraction, cutoffs):
    cell_ids = jnp.arange(NLON, dtype=jnp.int32)
    per_cell = jnp.take(source, cell_ids // BLK, axis=1)
    source_row = per_cell // NBLK
    source_block = per_cell % NBLK
    anchor = (source_row * NLON + source_block * BLK + offset).astype(jnp.int32)
    polar_rows = jnp.concatenate([jnp.arange(PROWS, dtype=jnp.int32), NLAT - PROWS + jnp.arange(PROWS, dtype=jnp.int32)])
    wavenumbers = jnp.arange(NLON // 2 + 1, dtype=jnp.int32)
    cutoff_values = cutoffs.reshape(2 * PROWS).astype(jnp.float32)
    ratios = cutoff_values[:, None] / jnp.maximum(wavenumbers, 1).astype(jnp.float32)[None, :]
    inside = (wavenumbers >= 1) & (wavenumbers < NLON // 2)
    damping = jnp.where(inside[None, :], jnp.maximum(1.0 - ratios, 0.0), 0.0)

    def advect(channel_field):
        flat_values = channel_field.reshape(-1)
        limited = cubic_limited(flat_values[anchor - 1], flat_values[anchor], flat_values[anchor + 1], flat_values[anchor + 2], fraction)
        polar_band = limited[polar_rows]
        spectrum = jnp.fft.rfft(polar_band, axis=-1)
        removed = jnp.fft.irfft(spectrum * damping, n=NLON, axis=-1)
        return limited.at[polar_rows].set(polar_band - removed.astype(polar_band.dtype))

    return lax.map(advect, tracer)
```

```python
import math

import jax
import jax.numpy as jnp
import ml_dtypes
import numpy as np
from jax import lax
from jax.experimental import pallas as pl
from jax.experimental.pallas import tpu as pltpu
from jax.sharding import PartitionSpec as P

NLON = 2048
BLK = 128
NBLK = NLON // BLK
HL = 2
PROWS = 8
PADDED = 40
F32 = jnp.float32
BF16 = jnp.bfloat16


def cubic_weights(position):
    return (
        -position * (position - 1.0) * (position - 2.0) / 6.0,
        (position + 1.0) * (position - 1.0) * (position - 2.0) / 2.0,
        -(position + 1.0) * position * (position - 2.0) / 2.0,
        (position + 1.0) * position * (position - 1.0) / 6.0,
    )


def cubic_limited(values, cells, weights):
    def at(shift):
        return jnp.take_along_axis(values, cells + shift, axis=1, mode="promise_in_bounds")

    before_one, at_anchor, after_one, after_two = at(-1), at(0), at(1), at(2)
    interpolated = (
        weights[0] * before_one
        + weights[1] * at_anchor
        + weights[2] * after_one
        + weights[3] * after_two
    )
    lowest_bound = jnp.minimum(at_anchor, after_one)
    upper_bound = jnp.maximum(at_anchor, after_one)
    return jnp.minimum(jnp.maximum(interpolated, lowest_bound), upper_bound)


def two_pieces(table):
    high = table.astype(ml_dtypes.bfloat16)
    return high, (table - high.astype(np.float64)).astype(ml_dtypes.bfloat16)


def fourier_tables():
    b = np.arange(NBLK)
    angles = 2.0 * math.pi * np.outer(b, b) / NBLK
    rows = np.eye(PROWS)
    blocks = np.concatenate([np.kron(np.cos(angles), rows), -np.kron(np.sin(angles), rows)], 0)
    i = np.arange(BLK)
    angles = 2.0 * math.pi * (np.outer(i, i) % BLK) / BLK
    cosine, sine = np.cos(angles), np.sin(angles)
    cells = np.block([[cosine, -sine], [sine, cosine]])
    angles = 2.0 * math.pi * np.repeat(np.outer(b, i), PROWS, 0) / NLON
    turn = np.stack([np.cos(angles), -np.sin(angles)]).astype(np.float32)
    return (*two_pieces(blocks), *two_pieces(blocks.T.copy()), *two_pieces(cells), turn)


def dot(left, right):
    return jnp.dot(left, right, preferred_element_type=F32)


def split(values):
    high = values.astype(BF16)
    return high, (values - high.astype(F32)).astype(BF16)


def pack_kernel(first_ref, tracer, source, offset, fraction, out):
    first = pl.multiple_of(first_ref[0], PROWS)
    rows = pl.ds(first, PROWS)
    anchor = source[rows, :] * BLK + offset[rows, :]
    channels = tracer.shape[0]
    out[:, 0:2] = tracer[:, rows, :].reshape(NBLK, channels // NBLK, PROWS, BLK)
    shape = (NBLK, PROWS, BLK)
    out[:, 2] = jnp.broadcast_to(anchor.astype(F32), shape)
    out[:, 3] = jnp.broadcast_to(fraction[rows, :], shape)


def polar_kernel(
    band, weights, blocks_h, blocks_l, back_h, back_l, cells_h, cells_l, turn, out
):
    count = NBLK * PROWS
    anchor = band[:, 2].reshape(count, BLK).astype(jnp.int32)
    place = ((anchor >> 7) & 15) * PROWS + ((anchor >> 11) & 7)
    lanes = lax.broadcasted_iota(jnp.int32, (count, BLK), 1)
    chosen = jnp.where(place == lanes, 1.0, 0.0).astype(BF16)
    own = jnp.concatenate([band[:, 0].reshape(count, BLK), band[:, 1].reshape(count, BLK)], 1)
    high = own.astype(BF16)
    rest = own - high.astype(F32)
    middle = rest.astype(BF16)
    low = (rest - middle.astype(F32)).astype(BF16)
    picked = dot(chosen, high) + dot(chosen, middle) + dot(chosen, low)
    cell = anchor & 127
    cubic = cubic_weights(band[:, 3].reshape(count, BLK))
    limited = [
        cubic_limited(picked[:, :BLK], cell, cubic),
        cubic_limited(picked[:, BLK:], cell, cubic),
    ]
    turn_r, turn_i = turn[0], turn[1]
    high, low = split(jnp.concatenate(limited, 1))
    first = dot(blocks_h[...], high) + dot(blocks_h[...], low) + dot(blocks_l[...], high)
    parts = []
    for c in range(2):
        real, imag = first[:count, c * BLK : (c + 1) * BLK], first[count:, c * BLK : (c + 1) * BLK]
        parts.append(
            jnp.concatenate([real * turn_r - imag * turn_i, real * turn_i + imag * turn_r], 1)
        )
    high, low = split(jnp.concatenate(parts, 0))
    spectrum = dot(high, cells_h[...]) + dot(low, cells_h[...]) + dot(high, cells_l[...])
    damping = jnp.concatenate([weights[...], weights[...]], 0)
    damped = jnp.concatenate([spectrum[:, BLK:] * damping, spectrum[:, :BLK] * damping], 1)
    high, low = split(damped)
    second = dot(high, cells_h[...]) + dot(low, cells_h[...]) + dot(high, cells_l[...])
    reals, imags = [], []
    for c in range(2):
        imag, real = second[c * count : (c + 1) * count, :BLK], second[c * count : (c + 1) * count, BLK:]
        reals.append(real * turn_r + imag * turn_i)
        imags.append(imag * turn_r - real * turn_i)
    high, low = split(
        jnp.concatenate([jnp.concatenate(reals, 1), jnp.concatenate(imags, 1)], 0)
    )
    removed = dot(back_h[...], high) + dot(back_h[...], low) + dot(back_l[...], high)
    for c in range(2):
        kept = limited[c] - removed[:, c * BLK : (c + 1) * BLK]
        out[:, c] = kept.reshape(NBLK, PROWS, BLK)


def rows_kernel(
    place, offset, fraction, own, west, east, halo, halo_west, halo_east, out, field, cubic, sems
):
    channels, rows = own.shape[0], own.shape[1]
    span = channels * PADDED
    columns = field.reshape(3, channels, PADDED, BLK)
    copies = [
        pltpu.make_async_copy(part, columns.at[n, :, pl.ds(0, rows), :], sems.at[n])
        for n, part in enumerate((west, own, east))
    ]
    for copy in copies:
        copy.start()
    for n, part in enumerate((halo_west, halo, halo_east)):
        columns[n, :, rows : rows + 2 * HL, :] = part[...]
    for n, weight in enumerate(cubic_weights(fraction[...])):
        cubic[n] = weight
    for copy in copies:
        copy.wait()
    flat_out = out.reshape(channels * rows, BLK)
    for j in range(rows):
        values = field[pl.ds(place[j], channels, stride=PADDED), :]
        cells = jnp.broadcast_to(offset[j : j + 1, :], (channels, BLK))
        weights = [cubic[n, j : j + 1, :] for n in range(4)]
        flat_out[pl.ds(j, channels, stride=rows), :] = cubic_limited(values, cells, weights)


def merge_kernel(first_ref, polar_ref, rows_done, polar, out, sem):
    @pl.when(polar_ref[0] == 1)
    def _():
        first = pl.multiple_of(first_ref[0], PROWS)
        copy = pltpu.make_async_copy(polar, out.at[:, pl.ds(first, PROWS), :], sem)
        copy.start()
        copy.wait()


def body(tracer, source, offset, fraction, cutoffs):
    channels, rows, cells = tracer.shape
    lat_count = lax.axis_size("lat")
    lat, lon = lax.axis_index("lat"), lax.axis_index("lon")
    first_row = lat * rows
    slab = jnp.where(lat == 0, 0, rows - PROWS).astype(jnp.int32).reshape(1)
    is_polar = ((lat == 0) | (lat == lat_count - 1)).astype(jnp.int32).reshape(1)

    smem = pl.BlockSpec(memory_space=pltpu.SMEM)
    vmem = pl.BlockSpec(memory_space=pltpu.VMEM)
    anyplace = pl.BlockSpec(memory_space=pl.ANY)

    with jax.named_scope("pack_polar_band"):
        packed = pl.pallas_call(
            pack_kernel,
            out_shape=jax.ShapeDtypeStruct((NBLK, 4, PROWS, BLK), F32),
            in_specs=[smem, vmem, vmem, vmem, vmem],
            out_specs=vmem,
            compiler_params=pltpu.CompilerParams(vmem_limit_bytes=8 << 20),
            cost_estimate=pl.CostEstimate(flops=0, bytes_accessed=1 << 20, transcendentals=0),
        )(slab, tracer, source, offset, fraction)

    with jax.named_scope("halos"):
        up = [(n, n + 1) for n in range(lat_count - 1)]
        down = [(n + 1, n) for n in range(lat_count - 1)]
        around = [(n, (n + 1) % NBLK) for n in range(NBLK)]
        back = [((n + 1) % NBLK, n) for n in range(NBLK)]
        west = lax.ppermute(tracer, "lon", around)
        east = lax.ppermute(tracer, "lon", back)
        north = lax.ppermute(tracer[:, rows - HL :, :], "lat", up)
        south = lax.ppermute(tracer[:, :HL, :], "lat", down)
        halo = jnp.concatenate([north, south], 1)
        halo_west = lax.ppermute(halo, "lon", around)
        halo_east = lax.ppermute(halo, "lon", back)

    with jax.named_scope("polar_rows"):
        band = lax.all_to_all(packed, "lon", 0, 0)
        kappa = jnp.where(lat == 0, cutoffs[0], cutoffs[1]).astype(F32)
        k1 = jnp.arange(NBLK, dtype=jnp.int32)
        k2 = jnp.arange(BLK, dtype=jnp.int32)
        wave = k1[:, None, None] + NBLK * k2[None, None, :]
        wave = jnp.minimum(wave, NLON - wave)
        inside = (wave >= 1) & (wave < NLON // 2)
        ratio = kappa[None, :, None] / jnp.maximum(wave, 1).astype(F32)
        damping = jnp.where(inside, jnp.maximum(1.0 - ratio, 0.0), 0.0) * (1.0 / NLON)
        filtered = pl.pallas_call(
            polar_kernel,
            out_shape=jax.ShapeDtypeStruct((NBLK, 2, PROWS, BLK), F32),
            in_specs=[vmem] * 9,
            out_specs=vmem,
            compiler_params=pltpu.CompilerParams(vmem_limit_bytes=16 << 20),
            cost_estimate=pl.CostEstimate(
                flops=400_000_000, bytes_accessed=2 << 20, transcendentals=0
            ),
        )(band, damping.reshape(NBLK * PROWS, BLK), *fourier_tables())
        polar = lax.all_to_all(filtered, "lon", 0, 0).reshape(channels, PROWS, BLK)

    with jax.named_scope("other_rows"):
        row = source[:, 0] // NBLK - first_row
        row = jnp.where(row < 0, row + rows + HL, jnp.where(row >= rows, row + HL, row))
        row = jnp.clip(row, 0, rows + 2 * HL - 1)
        column = jnp.clip(jnp.mod(source[:, 0] % NBLK - lon + 1, NBLK), 0, 2)
        place = column * (channels * PADDED) + row
        done = pl.pallas_call(
            rows_kernel,
            out_shape=jax.ShapeDtypeStruct(tracer.shape, F32),
            in_specs=[smem, vmem, vmem, anyplace, anyplace, anyplace, vmem, vmem, vmem],
            out_specs=vmem,
            scratch_shapes=[
                pltpu.VMEM((3 * channels * PADDED, BLK), F32),
                pltpu.VMEM((4, rows, BLK), F32),
                pltpu.SemaphoreType.DMA((3,)),
            ],
            compiler_params=pltpu.CompilerParams(vmem_limit_bytes=16 << 20),
            cost_estimate=pl.CostEstimate(
                flops=4_000_000, bytes_accessed=8 << 20, transcendentals=0
            ),
        )(place, offset, fraction, tracer, west, east, halo, halo_west, halo_east)

    with jax.named_scope("merge"):
        return pl.pallas_call(
            merge_kernel,
            out_shape=jax.ShapeDtypeStruct(tracer.shape, F32),
            in_specs=[smem, smem, anyplace, anyplace],
            out_specs=anyplace,
            scratch_shapes=[pltpu.SemaphoreType.DMA],
            input_output_aliases={2: 0},
            compiler_params=pltpu.CompilerParams(vmem_limit_bytes=4 << 20),
        )(slab, is_polar, done, polar)


def solution(mesh):
    placed = (P(None, "lat", "lon"), P("lat", "lon"), P("lat", "lon"), P("lat", "lon"), P())
    return jax.shard_map(
        body, mesh=mesh, in_specs=placed, out_specs=P(None, "lat", "lon"), check_vma=False
    )
```

```python
import math

import jax
import jax.numpy as jnp
import ml_dtypes
import numpy as np
from jax import lax
from jax.experimental import pallas as pl
from jax.experimental.pallas import tpu as pltpu
from jax.sharding import PartitionSpec as P

NLON = 2048
BLK = 128
NBLK = NLON // BLK
HL = 2
PROWS = 8
F32 = jnp.float32
BF16 = jnp.bfloat16


def cubic_weights(position):
    return (
        -position * (position - 1.0) * (position - 2.0) / 6.0,
        (position + 1.0) * (position - 1.0) * (position - 2.0) / 2.0,
        -(position + 1.0) * position * (position - 2.0) / 2.0,
        (position + 1.0) * position * (position - 1.0) / 6.0,
    )


def cubic_limited(values, cells, weights):
    def at(shift):
        return jnp.take_along_axis(values, cells + shift, axis=1, mode="promise_in_bounds")

    before_one, at_anchor, after_one, after_two = at(-1), at(0), at(1), at(2)
    interpolated = (
        weights[0] * before_one
        + weights[1] * at_anchor
        + weights[2] * after_one
        + weights[3] * after_two
    )
    lowest_bound = jnp.minimum(at_anchor, after_one)
    upper_bound = jnp.maximum(at_anchor, after_one)
    return jnp.minimum(jnp.maximum(interpolated, lowest_bound), upper_bound)


def two_pieces(table):
    high = table.astype(ml_dtypes.bfloat16)
    return high, (table - high.astype(np.float64)).astype(ml_dtypes.bfloat16)


def fourier_tables():
    b = np.arange(NBLK)
    angles = 2.0 * math.pi * np.outer(b, b) / NBLK
    rows = np.eye(PROWS)
    blocks = np.concatenate([np.kron(np.cos(angles), rows), -np.kron(np.sin(angles), rows)], 0)
    i = np.arange(BLK)
    angles = 2.0 * math.pi * (np.outer(i, i) % BLK) / BLK
    cosine, sine = np.cos(angles), np.sin(angles)
    cells = np.block([[cosine, -sine], [sine, cosine]])
    angles = 2.0 * math.pi * np.repeat(np.outer(b, i), PROWS, 0) / NLON
    turn = np.stack([np.cos(angles), -np.sin(angles)]).astype(np.float32)
    return (*two_pieces(blocks), *two_pieces(blocks.T.copy()), *two_pieces(cells), turn)


def dot(left, right):
    return jnp.dot(left, right, preferred_element_type=F32)


def split(values):
    high = values.astype(BF16)
    return high, (values - high.astype(F32)).astype(BF16)


def pack_kernel(source, tracer, offset, fraction, out, block, slab, cells, aux, sems):
    channels, rows = tracer.shape[0], tracer.shape[1]
    first = jnp.where(lax.axis_index("lat") == 0, 0, rows - PROWS)
    own = pl.ds(pl.multiple_of(first, PROWS), PROWS)
    copies = [
        pltpu.make_async_copy(source, block, sems.at[0]),
        pltpu.make_async_copy(offset.at[own, :], cells, sems.at[1]),
        pltpu.make_async_copy(fraction.at[own, :], aux.at[0, 1], sems.at[2]),
        pltpu.make_async_copy(tracer.at[:, own, :], slab, sems.at[3]),
    ]
    for copy in copies:
        copy.start()
    for copy in copies[:3]:
        copy.wait()
    spread = jnp.broadcast_to(block[...], (PROWS, rows))
    row = first + lax.broadcasted_iota(jnp.int32, (PROWS, rows), 0)
    mine = row == lax.broadcasted_iota(jnp.int32, (PROWS, rows), 1)
    source_block = jnp.sum(jnp.where(mine, spread, 0), axis=1, keepdims=True)
    anchor = (source_block * BLK + cells[...]).astype(F32)
    position = aux[0, 1]
    for n in range(NBLK):
        aux[n, 0] = anchor
        aux[n, 1] = position
    beside = pltpu.make_async_copy(aux, out.at[:, 2:4], sems.at[4])
    beside.start()
    copies[3].wait()
    share = slab.reshape(NBLK, channels // NBLK, PROWS, BLK)
    band = pltpu.make_async_copy(share, out.at[:, 0:2], sems.at[5])
    band.start()
    beside.wait()
    band.wait()


def polar_kernel(
    band, weights, blocks_h, blocks_l, back_h, back_l, cells_h, cells_l, turn, out
):
    count = NBLK * PROWS
    anchor = band[:, 2].reshape(count, BLK).astype(jnp.int32)
    place = ((anchor >> 7) & 15) * PROWS + ((anchor >> 11) & 7)
    lanes = lax.broadcasted_iota(jnp.int32, (count, BLK), 1)
    chosen = jnp.where(place == lanes, 1.0, 0.0).astype(BF16)
    own = jnp.concatenate([band[:, 0].reshape(count, BLK), band[:, 1].reshape(count, BLK)], 1)
    high = own.astype(BF16)
    rest = own - high.astype(F32)
    middle = rest.astype(BF16)
    low = (rest - middle.astype(F32)).astype(BF16)
    picked = dot(chosen, high) + dot(chosen, middle) + dot(chosen, low)
    cell = anchor & 127
    cubic = cubic_weights(band[:, 3].reshape(count, BLK))
    limited = [
        cubic_limited(picked[:, :BLK], cell, cubic),
        cubic_limited(picked[:, BLK:], cell, cubic),
    ]
    turn_r, turn_i = turn[0], turn[1]
    high, low = split(jnp.concatenate(limited, 1))
    first = dot(blocks_h[...], high) + dot(blocks_h[...], low) + dot(blocks_l[...], high)
    parts = []
    for c in range(2):
        real, imag = first[:count, c * BLK : (c + 1) * BLK], first[count:, c * BLK : (c + 1) * BLK]
        parts.append(
            jnp.concatenate([real * turn_r - imag * turn_i, real * turn_i + imag * turn_r], 1)
        )
    high, low = split(jnp.concatenate(parts, 0))
    spectrum = dot(high, cells_h[...]) + dot(low, cells_h[...]) + dot(high, cells_l[...])
    damping = jnp.concatenate([weights[...], weights[...]], 0)
    damped = jnp.concatenate([spectrum[:, BLK:] * damping, spectrum[:, :BLK] * damping], 1)
    high, low = split(damped)
    second = dot(high, cells_h[...]) + dot(low, cells_h[...]) + dot(high, cells_l[...])
    reals, imags = [], []
    for c in range(2):
        imag, real = second[c * count : (c + 1) * count, :BLK], second[c * count : (c + 1) * count, BLK:]
        reals.append(real * turn_r + imag * turn_i)
        imags.append(imag * turn_r - real * turn_i)
    high, low = split(
        jnp.concatenate([jnp.concatenate(reals, 1), jnp.concatenate(imags, 1)], 0)
    )
    removed = dot(back_h[...], high) + dot(back_h[...], low) + dot(back_l[...], high)
    for c in range(2):
        kept = limited[c] - removed[:, c * BLK : (c + 1) * BLK]
        out[:, c] = kept.reshape(NBLK, PROWS, BLK)


def column_rows(columns, first):
    channels, rows = columns[0].shape[0], columns[0].shape[1]
    flat = [column.reshape(channels * rows, BLK) for column in columns]
    return [part[pl.ds(first, channels, stride=rows), :] for part in flat]


def store_row(out, j, values):
    channels, rows = out.shape[0], out.shape[1]
    out.reshape(channels * rows, BLK)[pl.ds(j, channels, stride=rows), :] = values


def own_values(columns, column, row):
    west, own, east = column_rows(columns, jnp.clip(row, 0, columns[0].shape[1] - 1))
    return jnp.where(column == 0, west, jnp.where(column == 1, own, east))


def store_border(columns, lower, out):
    first = jnp.where(lower, columns[0].shape[1] - HL, 0)
    for j in range(HL):
        for n, values in enumerate(column_rows(columns, first + j)):
            out[n, j] = values


def border_kernel(west, own, east, out):
    store_border((west, own, east), lax.axis_index("lat") % 2 == 1, out)


def row_values(columns, column, row, beyond, halo):
    beyond = jnp.clip(beyond, 0, HL - 1)
    outside = (row < 0) | (row >= columns[0].shape[1])
    return jnp.where(outside, halo[column, beyond], own_values(columns, column, row))


def rows_kernel(place, offset, fraction, west, own, east, other, out, to_pair, cubic):
    first_of_pair = lax.axis_index("lat") % 2 == 0
    channels, rows = own.shape[0], own.shape[1]
    columns = (west, own, east)
    store_border(columns, first_of_pair, to_pair)
    for n, weight in enumerate(cubic_weights(fraction[...])):
        cubic[n] = weight
    for j in range(rows):
        column, row = place[0, j], place[1, j]
        if HL <= j < rows - HL:
            values = own_values(columns, column, row)
        else:
            values = row_values(columns, column, row, row + HL if j < HL else row - rows, other)
        cells = jnp.broadcast_to(offset[j : j + 1, :], (channels, BLK))
        weights = [cubic[n, j : j + 1, :] for n in range(4)]
        store_row(out, j, cubic_limited(values, cells, weights))


def edge_kernel(place, offset, fraction, west, own, east, pair, rows_done, out):
    del rows_done
    first_of_pair = lax.axis_index("lat") % 2 == 0
    channels, rows = own.shape[0], own.shape[1]
    first = jnp.where(first_of_pair, rows - HL, 0)
    for j in range(HL):
        column, row = place[0, first + j], place[1, first + j]
        beyond = jnp.where(first_of_pair, row - rows, row + HL)
        values = row_values((west, own, east), column, row, beyond, pair)
        here = pl.ds(first + j, 1)
        cells = jnp.broadcast_to(offset[here, :], (channels, BLK))
        store_row(out, first + j, cubic_limited(values, cells, cubic_weights(fraction[here, :])))


def merge_kernel(rows_done, polar, out, sems):
    lat = lax.axis_index("lat")
    last = lax.axis_size("lat") - 1
    rows = out.shape[1]

    def copy(source, first, count, n):
        span = pl.ds(first, count)
        part = source if source is polar else source.at[:, span, :]
        return pltpu.make_async_copy(part, out.at[:, span, :], sems.at[n])

    middle = copy(rows_done, PROWS, rows - 2 * PROWS, 0)
    middle.start()
    for n, (first, side) in enumerate(((0, 0), (rows - PROWS, last))):

        @pl.when(lat == side)
        def _():
            copy(polar, first, PROWS, n + 1).start()

        @pl.when(lat != side)
        def _():
            copy(rows_done, first, PROWS, n + 1).start()

    middle.wait()
    for n, first in enumerate((0, rows - PROWS)):
        copy(rows_done, first, PROWS, n + 1).wait()


def body(tracer, source, offset, fraction, cutoffs):
    channels, rows, cells = tracer.shape
    lat_count = lax.axis_size("lat")
    lat, lon = lax.axis_index("lat"), lax.axis_index("lon")
    blocks = source.reshape(rows)

    smem = pl.BlockSpec(memory_space=pltpu.SMEM)
    vmem = pl.BlockSpec(memory_space=pltpu.VMEM)
    anyplace = pl.BlockSpec(memory_space=pl.ANY)
    field = jax.ShapeDtypeStruct(tracer.shape, F32)

    def call(kernel, out_shape, in_specs, out_specs, scratch, limit, flops, **more):
        return pl.pallas_call(
            kernel,
            out_shape=out_shape,
            in_specs=in_specs,
            out_specs=out_specs,
            scratch_shapes=scratch,
            compiler_params=pltpu.CompilerParams(vmem_limit_bytes=limit << 20),
            cost_estimate=pl.CostEstimate(
                flops=flops, bytes_accessed=1 << 20, transcendentals=0
            ),
            **more,
        )

    def moved(values, target):
        pairs = []
        for a in range(lat_count):
            for b in range(NBLK):
                to = target(a, b)
                if 0 <= to[0] < lat_count:
                    pairs.append((a * NBLK + b, to[0] * NBLK + to[1] % NBLK))
        return lax.ppermute(values, ("lat", "lon"), pairs)

    dma = pltpu.SemaphoreType.DMA
    with jax.named_scope("lon_neighbours"):
        west = moved(tracer, lambda a, b: (a, b + 1))
        east = moved(tracer, lambda a, b: (a, b - 1))

    def filter_band():
        packed = call(
            pack_kernel,
            jax.ShapeDtypeStruct((NBLK, 4, PROWS, BLK), F32),
            [anyplace] * 4,
            anyplace,
            [
                pltpu.VMEM((1, rows), jnp.int32),
                pltpu.VMEM((channels, PROWS, BLK), F32),
                pltpu.VMEM((PROWS, BLK), jnp.int32),
                pltpu.VMEM((NBLK, 2, PROWS, BLK), F32),
                dma((6,)),
            ],
            60,
            1_000_000,
        )(source.reshape(1, rows), tracer, offset, fraction)
        band = lax.all_to_all(packed, "lon", 0, 0)
        kappa = jnp.where(lat == 0, cutoffs[0], cutoffs[1]).astype(F32)
        k1 = jnp.arange(NBLK, dtype=jnp.int32)
        k2 = jnp.arange(BLK, dtype=jnp.int32)
        wave = k1[:, None, None] + NBLK * k2[None, None, :]
        wave = jnp.minimum(wave, NLON - wave)
        inside = (wave >= 1) & (wave < NLON // 2)
        ratio = kappa[None, :, None] / jnp.maximum(wave, 1).astype(F32)
        damping = jnp.where(inside, jnp.maximum(1.0 - ratio, 0.0), 0.0) * (1.0 / NLON)
        return call(
            polar_kernel,
            jax.ShapeDtypeStruct((NBLK, 2, PROWS, BLK), F32),
            [vmem] * 9,
            vmem,
            [],
            16,
            400_000_000,
        )(band, damping.reshape(NBLK * PROWS, BLK), *fourier_tables())

    with jax.named_scope("polar_rows"):
        filtered = lax.cond(
            (lat == 0) | (lat == lat_count - 1),
            filter_band,
            lambda: jnp.zeros((NBLK, 2, PROWS, BLK), F32),
        )
        polar = lax.all_to_all(filtered, "lon", 0, 0).reshape(channels, PROWS, BLK)

    with jax.named_scope("borders"):
        border = jax.ShapeDtypeStruct((3, HL, channels, cells), F32)
        to_other = call(border_kernel, border, [vmem] * 3, vmem, [], 16, 1_000_000)(
            west, tracer, east
        )
        other = moved(to_other, lambda a, b: (a + (1 if a % 2 else -1), b))

    with jax.named_scope("other_rows"):
        row = blocks // NBLK - lat * rows
        column = jnp.clip(jnp.mod(blocks % NBLK - lon + 1, NBLK), 0, 2)
        place = jnp.stack([column, row])
        inner_done, to_pair = call(
            rows_kernel,
            (field, border),
            [smem] + [vmem] * 6,
            (vmem, vmem),
            [pltpu.VMEM((4, rows, BLK), F32)],
            16,
            3_000_000_000,
        )(place, offset, fraction, west, tracer, east, other)
        pair = moved(to_pair, lambda a, b: (a + (-1 if a % 2 else 1), b))
        done = call(
            edge_kernel,
            field,
            [smem] + [vmem] * 7,
            vmem,
            [],
            16,
            1_000_000,
            input_output_aliases={7: 0},
        )(place, offset, fraction, west, tracer, east, pair, inner_done)

    with jax.named_scope("merge"):
        return call(
            merge_kernel,
            field,
            [anyplace, anyplace],
            anyplace,
            [dma((3,))],
            4,
            1_000_000,
        )(done, polar)


def solution(mesh):
    placed = (P(None, "lat", "lon"), P("lat", "lon"), P("lat", "lon"), P("lat", "lon"), P())
    return jax.shard_map(
        body, mesh=mesh, in_specs=placed, out_specs=P(None, "lat", "lon"), check_vma=False
    )
```

```python
import math

import jax
import jax.numpy as jnp
import ml_dtypes
import numpy as np
from jax import lax
from jax.experimental import pallas as pl
from jax.experimental.pallas import tpu as pltpu
from jax.sharding import PartitionSpec as P

NLON = 2048
BLK = 128
NBLK = NLON // BLK
HL = 2
HALF = NBLK // 2 + 1
PROWS = 8
F32 = jnp.float32
BF16 = jnp.bfloat16


def cubic_weights(position):
    return (
        -position * (position - 1.0) * (position - 2.0) / 6.0,
        (position + 1.0) * (position - 1.0) * (position - 2.0) / 2.0,
        -(position + 1.0) * position * (position - 2.0) / 2.0,
        (position + 1.0) * position * (position - 1.0) / 6.0,
    )


def cubic_limited(values, cells, weights):
    def at(shift):
        return jnp.take_along_axis(values, cells + shift, axis=1, mode="promise_in_bounds")

    before_one, at_anchor, after_one, after_two = at(-1), at(0), at(1), at(2)
    interpolated = (
        weights[0] * before_one
        + weights[1] * at_anchor
        + weights[2] * after_one
        + weights[3] * after_two
    )
    lowest_bound = jnp.minimum(at_anchor, after_one)
    upper_bound = jnp.maximum(at_anchor, after_one)
    return jnp.minimum(jnp.maximum(interpolated, lowest_bound), upper_bound)


def two_pieces(table):
    high = table.astype(ml_dtypes.bfloat16)
    return np.stack([high, (table - high.astype(np.float64)).astype(ml_dtypes.bfloat16)])


def fourier_tables():
    b, k1 = np.arange(NBLK), np.arange(HALF)
    angles = 2.0 * math.pi * np.outer(k1, b) / NBLK
    rows = np.eye(PROWS)
    blocks = np.concatenate([np.kron(np.cos(angles), rows), -np.kron(np.sin(angles), rows)], 0)
    twice = np.where((k1 == 0) | (k1 == NBLK // 2), 1.0, 2.0)
    back = blocks.T * np.tile(np.repeat(twice, PROWS), 2)[None, :]
    i = np.arange(BLK)
    angles = 2.0 * math.pi * (np.outer(i, i) % BLK) / BLK
    cosine, sine = np.cos(angles), np.sin(angles)
    cells = np.block([[cosine, -sine], [sine, cosine]])
    angles = 2.0 * math.pi * np.repeat(np.outer(k1, i), PROWS, 0) / NLON
    turn = np.stack([np.cos(angles), -np.sin(angles)]).astype(np.float32)
    return two_pieces(blocks), two_pieces(back), two_pieces(cells), turn


def dot(left, right):
    return jnp.dot(left, right, preferred_element_type=F32)


def split(values):
    high = values.astype(BF16)
    return high, (values - high.astype(F32)).astype(BF16)


def pack_kernel(source, tracer, offset, fraction, out, block, slab, cells, aux, sems):
    channels, rows = tracer.shape[0], tracer.shape[1]
    first = jnp.where(lax.axis_index("lat") == 0, 0, rows - PROWS)
    own = pl.ds(pl.multiple_of(first, PROWS), PROWS)
    copies = [
        pltpu.make_async_copy(source, block, sems.at[0]),
        pltpu.make_async_copy(offset.at[own, :], cells, sems.at[1]),
        pltpu.make_async_copy(fraction.at[own, :], aux.at[0, 1], sems.at[2]),
        pltpu.make_async_copy(tracer.at[:, own, :], slab, sems.at[3]),
    ]
    for copy in copies:
        copy.start()
    for copy in copies[:3]:
        copy.wait()
    spread = jnp.broadcast_to(block[...], (PROWS, rows))
    row = first + lax.broadcasted_iota(jnp.int32, (PROWS, rows), 0)
    mine = row == lax.broadcasted_iota(jnp.int32, (PROWS, rows), 1)
    source_block = jnp.sum(jnp.where(mine, spread, 0), axis=1, keepdims=True)
    anchor = (source_block * BLK + cells[...]).astype(F32)
    position = aux[0, 1]
    for n in range(NBLK):
        aux[n, 0] = anchor
        aux[n, 1] = position
    beside = pltpu.make_async_copy(aux, out.at[:, 2:4], sems.at[4])
    beside.start()
    copies[3].wait()
    share = slab.reshape(NBLK, channels // NBLK, PROWS, BLK)
    band = pltpu.make_async_copy(share, out.at[:, 0:2], sems.at[5])
    band.start()
    beside.wait()
    band.wait()


def prepare_kernel(cutoffs, *refs):
    tables, damping, held = refs[:4], refs[4], refs[5:]
    for table, copy in zip(tables, held):
        copy[...] = table[...]
    shape = (HALF * PROWS, BLK)
    row = lax.broadcasted_iota(jnp.int32, shape, 0)
    wave = (row >> 3) + NBLK * lax.broadcasted_iota(jnp.int32, shape, 1)
    wave = jnp.minimum(wave, NLON - wave)
    side = jnp.where(lax.axis_index("lat") == 0, 0, 1)
    kappa = jnp.zeros(shape, jnp.int32)
    for j in range(PROWS):
        kappa = jnp.where((row & (PROWS - 1)) == j, cutoffs[side, j], kappa)
    inside = (wave >= 1) & (wave < NLON // 2)
    ratio = kappa.astype(F32) / jnp.maximum(wave, 1).astype(F32)
    damping[...] = jnp.where(inside, jnp.maximum(1.0 - ratio, 0.0), 0.0) * (1.0 / NLON)


def polar_kernel(band, weights, blocks, back, cells, turn, out):
    blocks_h, blocks_l = blocks[0], blocks[1]
    back_h, back_l = back[0], back[1]
    cells_h, cells_l = cells[0], cells[1]
    count = NBLK * PROWS
    half = HALF * PROWS
    anchor = band[:, 2].reshape(count, BLK).astype(jnp.int32)
    place = ((anchor >> 7) & 15) * PROWS + ((anchor >> 11) & 7)
    lanes = lax.broadcasted_iota(jnp.int32, (count, BLK), 1)
    chosen = jnp.where(place == lanes, 1.0, 0.0).astype(BF16)
    own = jnp.concatenate([band[:, 0].reshape(count, BLK), band[:, 1].reshape(count, BLK)], 1)
    high = own.astype(BF16)
    rest = own - high.astype(F32)
    middle = rest.astype(BF16)
    low = (rest - middle.astype(F32)).astype(BF16)
    picked = dot(chosen, high) + dot(chosen, middle) + dot(chosen, low)
    cell = anchor & 127
    cubic = cubic_weights(band[:, 3].reshape(count, BLK))
    limited = [
        cubic_limited(picked[:, :BLK], cell, cubic),
        cubic_limited(picked[:, BLK:], cell, cubic),
    ]
    turn_r, turn_i = turn[0], turn[1]
    high, low = split(jnp.concatenate(limited, 1))
    first = dot(blocks_h, high) + dot(blocks_h, low) + dot(blocks_l, high)
    parts = []
    for c in range(2):
        real, imag = first[:half, c * BLK : (c + 1) * BLK], first[half:, c * BLK : (c + 1) * BLK]
        parts.append(
            jnp.concatenate([real * turn_r - imag * turn_i, real * turn_i + imag * turn_r], 1)
        )
    high, low = split(jnp.concatenate(parts, 0))
    spectrum = dot(high, cells_h) + dot(low, cells_h) + dot(high, cells_l)
    damping = jnp.concatenate([weights[...], weights[...]], 0)
    damped = jnp.concatenate([spectrum[:, BLK:] * damping, spectrum[:, :BLK] * damping], 1)
    high, low = split(damped)
    second = dot(high, cells_h) + dot(low, cells_h) + dot(high, cells_l)
    reals, imags = [], []
    for c in range(2):
        imag, real = second[c * half : (c + 1) * half, :BLK], second[c * half : (c + 1) * half, BLK:]
        reals.append(real * turn_r + imag * turn_i)
        imags.append(imag * turn_r - real * turn_i)
    high, low = split(
        jnp.concatenate([jnp.concatenate(reals, 1), jnp.concatenate(imags, 1)], 0)
    )
    removed = dot(back_h, high) + dot(back_h, low) + dot(back_l, high)
    for c in range(2):
        kept = limited[c] - removed[:, c * BLK : (c + 1) * BLK]
        out[:, c] = kept.reshape(NBLK, PROWS, BLK)


def column_rows(columns, first):
    channels, rows = columns[0].shape[0], columns[0].shape[1]
    flat = [column.reshape(channels * rows, BLK) for column in columns]
    return [part[pl.ds(first, channels, stride=rows), :] for part in flat]


def store_row(out, j, values):
    channels, rows = out.shape[0], out.shape[1]
    out.reshape(channels * rows, BLK)[pl.ds(j, channels, stride=rows), :] = values


def own_values(columns, column, row):
    west, own, east = column_rows(columns, jnp.clip(row, 0, columns[0].shape[1] - 1))
    return jnp.where(column == 0, west, jnp.where(column == 1, own, east))


def border_kernel(west, own, east, *refs):
    out = refs[-1]
    to_other = len(refs) == 1
    rows = own.shape[1]
    lower = (lax.axis_index("lat") % 2 == 1) == to_other
    first = jnp.where(lower, rows - HL, 0)
    for j in range(HL):
        for n, values in enumerate(column_rows((west, own, east), first + j)):
            out[n, j] = values


def row_values(columns, column, row, beyond, halo):
    beyond = jnp.clip(beyond, 0, HL - 1)
    outside = (row < 0) | (row >= columns[0].shape[1])
    return jnp.where(outside, halo(column, beyond), own_values(columns, column, row))


def rows_kernel(place, offset, fraction, west, own, east, other, pair, out, cubic):
    first_of_pair = lax.axis_index("lat") % 2 == 0
    channels, rows = own.shape[0], own.shape[1]
    columns = (west, own, east)
    for n, weight in enumerate(cubic_weights(fraction[...])):
        cubic[n] = weight

    def north(column, row):
        return jnp.where(first_of_pair, other[column, row], pair[column, row])

    def south(column, row):
        return jnp.where(first_of_pair, pair[column, row], other[column, row])

    for j in range(rows):
        column, row = place[0, j], place[1, j]
        if j < HL:
            values = row_values(columns, column, row, row + HL, north)
        elif j < rows - HL:
            values = own_values(columns, column, row)
        else:
            values = row_values(columns, column, row, row - rows, south)
        cells = jnp.broadcast_to(offset[j : j + 1, :], (channels, BLK))
        weights = [cubic[n, j : j + 1, :] for n in range(4)]
        store_row(out, j, cubic_limited(values, cells, weights))


def merge_kernel(rows_done, polar, out, sem):
    lat = lax.axis_index("lat")
    last = lax.axis_size("lat") - 1

    @pl.when((lat == 0) | (lat == last))
    def _():
        first = pl.multiple_of(jnp.where(lat == 0, 0, out.shape[1] - PROWS), PROWS)
        copy = pltpu.make_async_copy(polar, out.at[:, pl.ds(first, PROWS), :], sem)
        copy.start()
        copy.wait()


def body(tracer, source, offset, fraction, cutoffs):
    channels, rows, cells = tracer.shape
    lat_count = lax.axis_size("lat")
    lat, lon = lax.axis_index("lat"), lax.axis_index("lon")
    blocks = source.reshape(rows)

    smem = pl.BlockSpec(memory_space=pltpu.SMEM)
    vmem = pl.BlockSpec(memory_space=pltpu.VMEM)
    anyplace = pl.BlockSpec(memory_space=pl.ANY)
    field = jax.ShapeDtypeStruct(tracer.shape, F32)

    def call(kernel, out_shape, in_specs, out_specs, scratch, limit, flops, **more):
        return pl.pallas_call(
            kernel,
            out_shape=out_shape,
            in_specs=in_specs,
            out_specs=out_specs,
            scratch_shapes=scratch,
            compiler_params=pltpu.CompilerParams(vmem_limit_bytes=limit << 20),
            cost_estimate=pl.CostEstimate(
                flops=flops, bytes_accessed=1 << 20, transcendentals=0
            ),
            **more,
        )

    def moved(values, target):
        pairs = []
        for a in range(lat_count):
            for b in range(NBLK):
                to = target(a, b)
                if 0 <= to[0] < lat_count:
                    pairs.append((a * NBLK + b, to[0] * NBLK + to[1] % NBLK))
        return lax.ppermute(values, ("lat", "lon"), pairs)

    dma = pltpu.SemaphoreType.DMA
    with jax.named_scope("lon_neighbours"):
        west = moved(tracer, lambda a, b: (a, b + 1))
        east = moved(tracer, lambda a, b: (a, b - 1))

    with jax.named_scope("pack_polar_band"):
        packed = call(
            pack_kernel,
            jax.ShapeDtypeStruct((NBLK, 4, PROWS, BLK), F32),
            [anyplace] * 4,
            anyplace,
            [
                pltpu.VMEM((1, rows), jnp.int32),
                pltpu.VMEM((channels, PROWS, BLK), F32),
                pltpu.VMEM((PROWS, BLK), jnp.int32),
                pltpu.VMEM((NBLK, 2, PROWS, BLK), F32),
                dma((6,)),
            ],
            60,
            1_000_000,
        )(source.reshape(1, rows), tracer, offset, fraction)

    def filter_band():
        band = lax.all_to_all(packed, "lon", 0, 0)
        tables = fourier_tables()
        damping = jax.ShapeDtypeStruct((HALF * PROWS, BLK), F32)
        held = [jax.ShapeDtypeStruct(table.shape, table.dtype) for table in tables]
        prepared = call(
            prepare_kernel,
            (damping, *held),
            [smem] + [vmem] * 4,
            (vmem,) * 5,
            [],
            16,
            1_000_000_000,
        )(cutoffs, *tables)
        return call(
            polar_kernel,
            jax.ShapeDtypeStruct((NBLK, 2, PROWS, BLK), F32),
            [vmem] * 6,
            vmem,
            [],
            16,
            400_000_000,
        )(band, *prepared)

    with jax.named_scope("polar_rows"):
        filtered = lax.cond(
            (lat == 0) | (lat == lat_count - 1),
            filter_band,
            lambda: jnp.zeros((NBLK, 2, PROWS, BLK), F32),
        )
        polar = lax.all_to_all(filtered, "lon", 0, 0).reshape(channels, PROWS, BLK)

    with jax.named_scope("borders"):
        border = jax.ShapeDtypeStruct((3, HL, channels, cells), F32)
        to_other = call(border_kernel, border, [vmem] * 3, vmem, [], 16, 1_000_000)(
            west, tracer, east
        )
        other = moved(to_other, lambda a, b: (a + (1 if a % 2 else -1), b))
        to_pair = call(border_kernel, border, [vmem] * 3 + [anyplace], vmem, [], 16, 1_000_000)(
            west, tracer, east, other
        )
        pair = moved(to_pair, lambda a, b: (a + (-1 if a % 2 else 1), b))

    with jax.named_scope("other_rows"):
        row = blocks // NBLK - lat * rows
        column = jnp.clip(jnp.mod(blocks % NBLK - lon + 1, NBLK), 0, 2)
        place = jnp.stack([column, row])
        done = call(
            rows_kernel,
            field,
            [smem] + [vmem] * 7,
            vmem,
            [pltpu.VMEM((4, rows, BLK), F32)],
            16,
            3_000_000_000,
        )(place, offset, fraction, west, tracer, east, other, pair)

    with jax.named_scope("merge"):
        return call(
            merge_kernel,
            field,
            [anyplace, anyplace],
            anyplace,
            [dma],
            4,
            1_000_000,
            input_output_aliases={0: 0},
        )(done, polar)


def solution(mesh):
    placed = (P(None, "lat", "lon"), P("lat", "lon"), P("lat", "lon"), P("lat", "lon"), P())
    return jax.shard_map(
        body, mesh=mesh, in_specs=placed, out_specs=P(None, "lat", "lon"), check_vma=False
    )
```

```python
import math

import jax
import jax.numpy as jnp
import ml_dtypes
import numpy as np
from jax import lax
from jax.experimental import pallas as pl
from jax.experimental.pallas import tpu as pltpu
from jax.sharding import PartitionSpec as P

NLON = 2048
BLK = 128
NBLK = NLON // BLK
HL = 2
HALF = NBLK // 2 + 1
PROWS = 8
F32 = jnp.float32
BF16 = jnp.bfloat16


def cubic_weights(position):
    return (
        -position * (position - 1.0) * (position - 2.0) / 6.0,
        (position + 1.0) * (position - 1.0) * (position - 2.0) / 2.0,
        -(position + 1.0) * position * (position - 2.0) / 2.0,
        (position + 1.0) * position * (position - 1.0) / 6.0,
    )


def cubic_limited(values, cells, weights):
    def at(shift):
        return jnp.take_along_axis(values, cells + shift, axis=1, mode="promise_in_bounds")

    before_one, at_anchor, after_one, after_two = at(-1), at(0), at(1), at(2)
    interpolated = (
        weights[0] * before_one
        + weights[1] * at_anchor
        + weights[2] * after_one
        + weights[3] * after_two
    )
    lowest_bound = jnp.minimum(at_anchor, after_one)
    upper_bound = jnp.maximum(at_anchor, after_one)
    return jnp.minimum(jnp.maximum(interpolated, lowest_bound), upper_bound)


def two_pieces(table):
    high = table.astype(ml_dtypes.bfloat16)
    return np.stack([high, (table - high.astype(np.float64)).astype(ml_dtypes.bfloat16)])


def fourier_tables():
    b, k1 = np.arange(NBLK), np.arange(HALF)
    angles = 2.0 * math.pi * np.outer(k1, b) / NBLK
    rows = np.eye(PROWS)
    blocks = np.concatenate([np.kron(np.cos(angles), rows), -np.kron(np.sin(angles), rows)], 0)
    twice = np.where((k1 == 0) | (k1 == NBLK // 2), 1.0, 2.0)
    back = blocks.T * np.tile(np.repeat(twice, PROWS), 2)[None, :]
    i = np.arange(BLK)
    angles = 2.0 * math.pi * (np.outer(i, i) % BLK) / BLK
    cosine, sine = np.cos(angles), np.sin(angles)
    cells = np.block([[cosine, -sine], [sine, cosine]])
    angles = 2.0 * math.pi * np.repeat(np.outer(k1, i), PROWS, 0) / NLON
    turn = np.stack([np.cos(angles), -np.sin(angles)]).astype(np.float32)
    return two_pieces(blocks), two_pieces(back), two_pieces(cells), turn


def dot(left, right):
    return jnp.dot(left, right, preferred_element_type=F32)


def split(values):
    high = values.astype(BF16)
    return high, (values - high.astype(F32)).astype(BF16)


def pack_kernel(source, tracer, offset, fraction, out, block, slab, cells, aux, sems):
    channels, rows = tracer.shape[0], tracer.shape[1]
    first = jnp.where(lax.axis_index("lat") == 0, 0, rows - PROWS)
    own = pl.ds(pl.multiple_of(first, PROWS), PROWS)
    copies = [
        pltpu.make_async_copy(source, block, sems.at[0]),
        pltpu.make_async_copy(offset.at[own, :], cells, sems.at[1]),
        pltpu.make_async_copy(fraction.at[own, :], aux.at[0, 1], sems.at[2]),
        pltpu.make_async_copy(tracer.at[:, own, :], slab, sems.at[3]),
    ]
    for copy in copies:
        copy.start()
    for copy in copies[:3]:
        copy.wait()
    spread = jnp.broadcast_to(block[...], (PROWS, rows))
    row = first + lax.broadcasted_iota(jnp.int32, (PROWS, rows), 0)
    mine = row == lax.broadcasted_iota(jnp.int32, (PROWS, rows), 1)
    source_block = jnp.sum(jnp.where(mine, spread, 0), axis=1, keepdims=True)
    anchor = (source_block * BLK + cells[...]).astype(F32)
    position = aux[0, 1]
    for n in range(NBLK):
        aux[n, 0] = anchor
        aux[n, 1] = position
    beside = pltpu.make_async_copy(aux, out.at[:, 2:4], sems.at[4])
    beside.start()
    copies[3].wait()
    share = slab.reshape(NBLK, channels // NBLK, PROWS, BLK)
    band = pltpu.make_async_copy(share, out.at[:, 0:2], sems.at[5])
    band.start()
    beside.wait()
    band.wait()


def prepare_kernel(cutoffs, *refs):
    tables, damping, held = refs[:4], refs[4], refs[5:]
    for table, copy in zip(tables, held):
        copy[...] = table[...]
    shape = (HALF * PROWS, BLK)
    row = lax.broadcasted_iota(jnp.int32, shape, 0)
    wave = (row >> 3) + NBLK * lax.broadcasted_iota(jnp.int32, shape, 1)
    wave = jnp.minimum(wave, NLON - wave)
    side = jnp.where(lax.axis_index("lat") == 0, 0, 1)
    kappa = jnp.zeros(shape, jnp.int32)
    for j in range(PROWS):
        kappa = jnp.where((row & (PROWS - 1)) == j, cutoffs[side, j], kappa)
    inside = (wave >= 1) & (wave < NLON // 2)
    ratio = kappa.astype(F32) / jnp.maximum(wave, 1).astype(F32)
    damping[...] = jnp.where(inside, jnp.maximum(1.0 - ratio, 0.0), 0.0) * (1.0 / NLON)


def polar_kernel(band, weights, blocks, back, cells, turn, out):
    blocks_h, blocks_l = blocks[0], blocks[1]
    back_h, back_l = back[0], back[1]
    cells_h, cells_l = cells[0], cells[1]
    count = NBLK * PROWS
    half = HALF * PROWS
    anchor = band[:, 2].reshape(count, BLK).astype(jnp.int32)
    place = ((anchor >> 7) & 15) * PROWS + ((anchor >> 11) & 7)
    lanes = lax.broadcasted_iota(jnp.int32, (count, BLK), 1)
    chosen = jnp.where(place == lanes, 1.0, 0.0).astype(BF16)
    own = jnp.concatenate([band[:, 0].reshape(count, BLK), band[:, 1].reshape(count, BLK)], 1)
    high = own.astype(BF16)
    rest = own - high.astype(F32)
    middle = rest.astype(BF16)
    low = (rest - middle.astype(F32)).astype(BF16)
    picked = dot(chosen, high) + dot(chosen, middle) + dot(chosen, low)
    cell = anchor & 127
    cubic = cubic_weights(band[:, 3].reshape(count, BLK))
    limited = [
        cubic_limited(picked[:, :BLK], cell, cubic),
        cubic_limited(picked[:, BLK:], cell, cubic),
    ]
    turn_r, turn_i = turn[0], turn[1]
    high, low = split(jnp.concatenate(limited, 1))
    first = dot(blocks_h, high) + dot(blocks_h, low) + dot(blocks_l, high)
    parts = []
    for c in range(2):
        real, imag = first[:half, c * BLK : (c + 1) * BLK], first[half:, c * BLK : (c + 1) * BLK]
        parts.append(
            jnp.concatenate([real * turn_r - imag * turn_i, real * turn_i + imag * turn_r], 1)
        )
    high, low = split(jnp.concatenate(parts, 0))
    spectrum = dot(high, cells_h) + dot(low, cells_h) + dot(high, cells_l)
    damping = jnp.concatenate([weights[...], weights[...]], 0)
    damped = jnp.concatenate([spectrum[:, BLK:] * damping, spectrum[:, :BLK] * damping], 1)
    high, low = split(damped)
    second = dot(high, cells_h) + dot(low, cells_h) + dot(high, cells_l)
    reals, imags = [], []
    for c in range(2):
        imag, real = second[c * half : (c + 1) * half, :BLK], second[c * half : (c + 1) * half, BLK:]
        reals.append(real * turn_r + imag * turn_i)
        imags.append(imag * turn_r - real * turn_i)
    high, low = split(
        jnp.concatenate([jnp.concatenate(reals, 1), jnp.concatenate(imags, 1)], 0)
    )
    removed = dot(back_h, high) + dot(back_h, low) + dot(back_l, high)
    for c in range(2):
        kept = limited[c] - removed[:, c * BLK : (c + 1) * BLK]
        out[:, c] = kept.reshape(NBLK, PROWS, BLK)


def column_rows(columns, first):
    channels, rows = columns[0].shape[0], columns[0].shape[1]
    flat = [column.reshape(channels * rows, BLK) for column in columns]
    return [part[pl.ds(first, channels, stride=rows), :] for part in flat]


def store_row(out, j, values):
    channels, rows = out.shape[0], out.shape[1]
    out.reshape(channels * rows, BLK)[pl.ds(j, channels, stride=rows), :] = values


def own_values(columns, column, row):
    west, own, east = column_rows(columns, jnp.clip(row, 0, columns[0].shape[1] - 1))
    return jnp.where(column == 0, west, jnp.where(column == 1, own, east))


def border_kernel(west, own, east, *refs):
    out = refs[-1]
    to_other = len(refs) == 1
    rows = own.shape[1]
    lower = (lax.axis_index("lat") % 2 == 1) == to_other
    first = jnp.where(lower, rows - HL, 0)
    for j in range(HL):
        for n, values in enumerate(column_rows((west, own, east), first + j)):
            out[n, j] = values


def row_values(columns, column, row, beyond, halo):
    beyond = jnp.clip(beyond, 0, HL - 1)
    outside = (row < 0) | (row >= columns[0].shape[1])
    return jnp.where(outside, halo(column, beyond), own_values(columns, column, row))


def rows_kernel(place, offset, fraction, west, own, east, other, pair, out, cubic):
    first_of_pair = lax.axis_index("lat") % 2 == 0
    channels, rows = own.shape[0], own.shape[1]
    columns = (west, own, east)
    for n, weight in enumerate(cubic_weights(fraction[...])):
        cubic[n] = weight

    def north(column, row):
        return jnp.where(first_of_pair, other[column, row], pair[column, row])

    def south(column, row):
        return jnp.where(first_of_pair, pair[column, row], other[column, row])

    for j in range(rows):
        column, row = place[0, j], place[1, j]
        if j < HL:
            values = row_values(columns, column, row, row + HL, north)
        elif j < rows - HL:
            values = own_values(columns, column, row)
        else:
            values = row_values(columns, column, row, row - rows, south)
        cells = jnp.broadcast_to(offset[j : j + 1, :], (channels, BLK))
        weights = [cubic[n, j : j + 1, :] for n in range(4)]
        store_row(out, j, cubic_limited(values, cells, weights))


def merge_kernel(rows_done, polar, out, sem):
    lat = lax.axis_index("lat")
    last = lax.axis_size("lat") - 1

    @pl.when((lat == 0) | (lat == last))
    def _():
        first = pl.multiple_of(jnp.where(lat == 0, 0, out.shape[1] - PROWS), PROWS)
        copy = pltpu.make_async_copy(polar, out.at[:, pl.ds(first, PROWS), :], sem)
        copy.start()
        copy.wait()


def return_groups(lat_count):
    last = lat_count - 1
    planes = [b + half for b in range(NBLK // 2) for half in (0, NBLK // 2)]
    others = [a * NBLK + b for b in planes for a in range(1, last)]
    ends = [[a * NBLK + b for b in range(NBLK)] for a in (0, last)]
    return ends + [others[n : n + NBLK] for n in range(0, len(others), NBLK)]


def body(tracer, source, offset, fraction, cutoffs):
    channels, rows, cells = tracer.shape
    lat_count = lax.axis_size("lat")
    lat, lon = lax.axis_index("lat"), lax.axis_index("lon")
    blocks = source.reshape(rows)

    smem = pl.BlockSpec(memory_space=pltpu.SMEM)
    vmem = pl.BlockSpec(memory_space=pltpu.VMEM)
    anyplace = pl.BlockSpec(memory_space=pl.ANY)
    field = jax.ShapeDtypeStruct(tracer.shape, F32)

    def call(kernel, out_shape, in_specs, out_specs, scratch, limit, flops, **more):
        return pl.pallas_call(
            kernel,
            out_shape=out_shape,
            in_specs=in_specs,
            out_specs=out_specs,
            scratch_shapes=scratch,
            compiler_params=pltpu.CompilerParams(vmem_limit_bytes=limit << 20),
            cost_estimate=pl.CostEstimate(
                flops=flops, bytes_accessed=1 << 20, transcendentals=0
            ),
            **more,
        )

    def moved(values, target):
        pairs = []
        for a in range(lat_count):
            for b in range(NBLK):
                to = target(a, b)
                if 0 <= to[0] < lat_count:
                    pairs.append((a * NBLK + b, to[0] * NBLK + to[1] % NBLK))
        return lax.ppermute(values, ("lat", "lon"), pairs)

    dma = pltpu.SemaphoreType.DMA
    with jax.named_scope("lon_neighbours"):
        west = moved(tracer, lambda a, b: (a, b + 1))
        east = moved(tracer, lambda a, b: (a, b - 1))

    with jax.named_scope("pack_polar_band"):
        packed = call(
            pack_kernel,
            jax.ShapeDtypeStruct((NBLK, 4, PROWS, BLK), F32),
            [anyplace] * 4,
            anyplace,
            [
                pltpu.VMEM((1, rows), jnp.int32),
                pltpu.VMEM((channels, PROWS, BLK), F32),
                pltpu.VMEM((PROWS, BLK), jnp.int32),
                pltpu.VMEM((NBLK, 2, PROWS, BLK), F32),
                dma((6,)),
            ],
            60,
            1_000_000,
        )(source.reshape(1, rows), tracer, offset, fraction)

    def filter_band():
        band = lax.all_to_all(packed, "lon", 0, 0)
        tables = fourier_tables()
        damping = jax.ShapeDtypeStruct((HALF * PROWS, BLK), F32)
        held = [jax.ShapeDtypeStruct(table.shape, table.dtype) for table in tables]
        prepared = call(
            prepare_kernel,
            (damping, *held),
            [smem] + [vmem] * 4,
            (vmem,) * 5,
            [],
            16,
            1_000_000_000,
        )(cutoffs, *tables)
        return call(
            polar_kernel,
            jax.ShapeDtypeStruct((NBLK, 2, PROWS, BLK), F32),
            [vmem] * 6,
            vmem,
            [],
            16,
            400_000_000,
        )(band, *prepared)

    with jax.named_scope("polar_rows"):
        filtered = lax.cond(
            (lat == 0) | (lat == lat_count - 1),
            filter_band,
            lambda: jnp.zeros((NBLK, 2, PROWS, BLK), F32),
        )
        polar = lax.all_to_all(
            filtered, ("lat", "lon"), 0, 0, axis_index_groups=return_groups(lat_count)
        ).reshape(channels, PROWS, BLK)

    with jax.named_scope("borders"):
        border = jax.ShapeDtypeStruct((3, HL, channels, cells), F32)
        to_other = call(border_kernel, border, [vmem] * 3, vmem, [], 16, 1_000_000)(
            west, tracer, east
        )
        other = moved(to_other, lambda a, b: (a + (1 if a % 2 else -1), b))
        to_pair = call(border_kernel, border, [vmem] * 3 + [anyplace], vmem, [], 16, 1_000_000)(
            west, tracer, east, other
        )
        pair = moved(to_pair, lambda a, b: (a + (-1 if a % 2 else 1), b))

    with jax.named_scope("other_rows"):
        row = blocks // NBLK - lat * rows
        column = jnp.clip(jnp.mod(blocks % NBLK - lon + 1, NBLK), 0, 2)
        place = jnp.stack([column, row])
        done = call(
            rows_kernel,
            field,
            [smem] + [vmem] * 7,
            vmem,
            [pltpu.VMEM((4, rows, BLK), F32)],
            16,
            3_000_000_000,
        )(place, offset, fraction, west, tracer, east, other, pair)

    with jax.named_scope("merge"):
        return call(
            merge_kernel,
            field,
            [anyplace, anyplace],
            anyplace,
            [dma],
            4,
            1_000_000,
            input_output_aliases={0: 0},
        )(done, polar)


def solution(mesh):
    placed = (P(None, "lat", "lon"), P("lat", "lon"), P("lat", "lon"), P("lat", "lon"), P())
    return jax.shard_map(
        body, mesh=mesh, in_specs=placed, out_specs=P(None, "lat", "lon"), check_vma=False
    )
```

```python
import math

import jax
import jax.numpy as jnp
import ml_dtypes
import numpy as np
from jax import lax
from jax.experimental import pallas as pl
from jax.experimental.pallas import tpu as pltpu
from jax.sharding import PartitionSpec as P

NLON = 2048
BLK = 128
NBLK = NLON // BLK
HL = 2
HALF = NBLK // 2 + 1
PROWS = 8
F32 = jnp.float32
BF16 = jnp.bfloat16


def cubic_weights(position):
    return (
        -position * (position - 1.0) * (position - 2.0) / 6.0,
        (position + 1.0) * (position - 1.0) * (position - 2.0) / 2.0,
        -(position + 1.0) * position * (position - 2.0) / 2.0,
        (position + 1.0) * position * (position - 1.0) / 6.0,
    )


def cubic_limited(values, cells, weights):
    def at(shift):
        return jnp.take_along_axis(values, cells + shift, axis=1, mode="promise_in_bounds")

    before_one, at_anchor, after_one, after_two = at(-1), at(0), at(1), at(2)
    interpolated = (
        weights[0] * before_one
        + weights[1] * at_anchor
        + weights[2] * after_one
        + weights[3] * after_two
    )
    lowest_bound = jnp.minimum(at_anchor, after_one)
    upper_bound = jnp.maximum(at_anchor, after_one)
    return jnp.minimum(jnp.maximum(interpolated, lowest_bound), upper_bound)


def three_products(table, axis):
    high = table.astype(ml_dtypes.bfloat16)
    low = (table - high.astype(np.float64)).astype(ml_dtypes.bfloat16)
    return np.concatenate([high, high, low], axis)


def fourier_tables():
    b, k1 = np.arange(NBLK), np.arange(HALF)
    angles = 2.0 * math.pi * np.outer(k1, b) / NBLK
    rows = np.eye(PROWS)
    blocks = np.concatenate([np.kron(np.cos(angles), rows), -np.kron(np.sin(angles), rows)], 0)
    twice = np.where((k1 == 0) | (k1 == NBLK // 2), 1.0, 2.0)
    back = blocks.T * np.tile(np.repeat(twice, PROWS), 2)[None, :]
    i = np.arange(BLK)
    angles = 2.0 * math.pi * (np.outer(i, i) % BLK) / BLK
    cosine, sine = np.cos(angles), np.sin(angles)
    cells = np.block([[cosine, -sine], [sine, cosine]])
    angles = 2.0 * math.pi * np.repeat(np.outer(k1, i), PROWS, 0) / NLON
    turn = np.stack([np.cos(angles), -np.sin(angles)]).astype(np.float32)
    return three_products(blocks, 1), three_products(back, 1), three_products(cells, 0), turn


def dot(left, right):
    return jnp.dot(left, right, preferred_element_type=F32)


def pieces(values, axis):
    high = values.astype(BF16)
    low = (values - high.astype(F32)).astype(BF16)
    return jnp.concatenate([high, low, high], axis)


def pack_kernel(source, tracer, offset, fraction, out, block, slab, cells, aux, sems):
    channels, rows = tracer.shape[0], tracer.shape[1]
    first = jnp.where(lax.axis_index("lat") == 0, 0, rows - PROWS)
    own = pl.ds(pl.multiple_of(first, PROWS), PROWS)
    copies = [
        pltpu.make_async_copy(source, block, sems.at[0]),
        pltpu.make_async_copy(offset.at[own, :], cells, sems.at[1]),
        pltpu.make_async_copy(fraction.at[own, :], aux.at[0, 1], sems.at[2]),
        pltpu.make_async_copy(tracer.at[:, own, :], slab, sems.at[3]),
    ]
    for copy in copies:
        copy.start()
    for copy in copies[:3]:
        copy.wait()
    spread = jnp.broadcast_to(block[...], (PROWS, rows))
    row = first + lax.broadcasted_iota(jnp.int32, (PROWS, rows), 0)
    mine = row == lax.broadcasted_iota(jnp.int32, (PROWS, rows), 1)
    source_block = jnp.sum(jnp.where(mine, spread, 0), axis=1, keepdims=True)
    anchor = (source_block * BLK + cells[...]).astype(F32)
    position = aux[0, 1]
    for n in range(NBLK):
        aux[n, 0] = anchor
        aux[n, 1] = position
    beside = pltpu.make_async_copy(aux, out.at[:, 2:4], sems.at[4])
    beside.start()
    copies[3].wait()
    share = slab.reshape(NBLK, channels // NBLK, PROWS, BLK)
    band = pltpu.make_async_copy(share, out.at[:, 0:2], sems.at[5])
    band.start()
    beside.wait()
    band.wait()


def prepare_kernel(cutoffs, *refs):
    tables, damping, held = refs[:4], refs[4], refs[5:]
    for table, copy in zip(tables, held):
        copy[...] = table[...]
    shape = (HALF * PROWS, BLK)
    row = lax.broadcasted_iota(jnp.int32, shape, 0)
    wave = (row >> 3) + NBLK * lax.broadcasted_iota(jnp.int32, shape, 1)
    wave = jnp.minimum(wave, NLON - wave)
    side = jnp.where(lax.axis_index("lat") == 0, 0, 1)
    kappa = jnp.zeros(shape, jnp.int32)
    for j in range(PROWS):
        kappa = jnp.where((row & (PROWS - 1)) == j, cutoffs[side, j], kappa)
    inside = (wave >= 1) & (wave < NLON // 2)
    ratio = kappa.astype(F32) / jnp.maximum(wave, 1).astype(F32)
    damping[...] = jnp.where(inside, jnp.maximum(1.0 - ratio, 0.0), 0.0) * (1.0 / NLON)


def polar_kernel(band, weights, blocks, back, cells, turn, out):
    count = NBLK * PROWS
    half = HALF * PROWS
    anchor = band[:, 2].reshape(count, BLK).astype(jnp.int32)
    place = ((anchor >> 7) & 15) * PROWS + ((anchor >> 11) & 7)
    lanes = lax.broadcasted_iota(jnp.int32, (count, BLK), 1)
    chosen = jnp.where(place == lanes, 1.0, 0.0).astype(BF16)
    own = jnp.concatenate([band[:, 0].reshape(count, BLK), band[:, 1].reshape(count, BLK)], 1)
    high = own.astype(BF16)
    rest = own - high.astype(F32)
    middle = rest.astype(BF16)
    low = (rest - middle.astype(F32)).astype(BF16)
    picked = dot(jnp.concatenate([chosen] * 3, 1), jnp.concatenate([high, middle, low], 0))
    cell = anchor & 127
    cubic = cubic_weights(band[:, 3].reshape(count, BLK))
    limited = [
        cubic_limited(picked[:, :BLK], cell, cubic),
        cubic_limited(picked[:, BLK:], cell, cubic),
    ]
    turn_r, turn_i = turn[0], turn[1]
    first = dot(blocks[...], pieces(jnp.concatenate(limited, 1), 0))
    parts = []
    for c in range(2):
        real, imag = first[:half, c * BLK : (c + 1) * BLK], first[half:, c * BLK : (c + 1) * BLK]
        parts.append(
            jnp.concatenate([real * turn_r - imag * turn_i, real * turn_i + imag * turn_r], 1)
        )
    spectrum = dot(pieces(jnp.concatenate(parts, 0), 1), cells[...])
    damping = jnp.concatenate([weights[...], weights[...]], 0)
    damped = jnp.concatenate([spectrum[:, BLK:] * damping, spectrum[:, :BLK] * damping], 1)
    second = dot(pieces(damped, 1), cells[...])
    reals, imags = [], []
    for c in range(2):
        imag, real = second[c * half : (c + 1) * half, :BLK], second[c * half : (c + 1) * half, BLK:]
        reals.append(real * turn_r + imag * turn_i)
        imags.append(imag * turn_r - real * turn_i)
    both = jnp.concatenate([jnp.concatenate(reals, 1), jnp.concatenate(imags, 1)], 0)
    removed = dot(back[...], pieces(both, 0))
    for c in range(2):
        kept = limited[c] - removed[:, c * BLK : (c + 1) * BLK]
        out[:, c] = kept.reshape(NBLK, PROWS, BLK)


def column_rows(columns, first):
    channels, rows = columns[0].shape[0], columns[0].shape[1]
    flat = [column.reshape(channels * rows, BLK) for column in columns]
    return [part[pl.ds(first, channels, stride=rows), :] for part in flat]


def store_row(out, j, values):
    channels, rows = out.shape[0], out.shape[1]
    out.reshape(channels * rows, BLK)[pl.ds(j, channels, stride=rows), :] = values


def own_values(columns, column, row):
    west, own, east = column_rows(columns, jnp.clip(row, 0, columns[0].shape[1] - 1))
    return jnp.where(column == 0, west, jnp.where(column == 1, own, east))


def border_kernel(west, own, east, *refs):
    out = refs[-1]
    to_other = len(refs) == 1
    rows = own.shape[1]
    lower = (lax.axis_index("lat") % 2 == 1) == to_other
    first = jnp.where(lower, rows - HL, 0)
    for j in range(HL):
        for n, values in enumerate(column_rows((west, own, east), first + j)):
            out[n, j] = values


def row_values(columns, column, row, beyond, halo):
    beyond = jnp.clip(beyond, 0, HL - 1)
    outside = (row < 0) | (row >= columns[0].shape[1])
    return jnp.where(outside, halo(column, beyond), own_values(columns, column, row))


def rows_kernel(place, offset, fraction, east, own, west, other, pair, out, cubic):
    first_of_pair = lax.axis_index("lat") % 2 == 0
    channels, rows = own.shape[0], own.shape[1]
    columns = (west, own, east)
    for n, weight in enumerate(cubic_weights(fraction[...])):
        cubic[n] = weight

    def north(column, row):
        return jnp.where(first_of_pair, other[column, row], pair[column, row])

    def south(column, row):
        return jnp.where(first_of_pair, pair[column, row], other[column, row])

    for j in range(rows):
        column, row = place[0, j], place[1, j]
        if j < HL:
            values = row_values(columns, column, row, row + HL, north)
        elif j < rows - HL:
            values = own_values(columns, column, row)
        else:
            values = row_values(columns, column, row, row - rows, south)
        cells = jnp.broadcast_to(offset[j : j + 1, :], (channels, BLK))
        weights = [cubic[n, j : j + 1, :] for n in range(4)]
        store_row(out, j, cubic_limited(values, cells, weights))


def merge_kernel(rows_done, polar, out, sem):
    lat = lax.axis_index("lat")
    last = lax.axis_size("lat") - 1

    @pl.when((lat == 0) | (lat == last))
    def _():
        first = pl.multiple_of(jnp.where(lat == 0, 0, out.shape[1] - PROWS), PROWS)
        copy = pltpu.make_async_copy(polar, out.at[:, pl.ds(first, PROWS), :], sem)
        copy.start()
        copy.wait()


def return_groups(lat_count):
    last = lat_count - 1
    planes = [b + half for b in range(NBLK // 2) for half in (0, NBLK // 2)]
    others = [a * NBLK + b for b in planes for a in range(1, last)]
    ends = [[a * NBLK + b for b in range(NBLK)] for a in (0, last)]
    return ends + [others[n : n + NBLK] for n in range(0, len(others), NBLK)]


def body(tracer, source, offset, fraction, cutoffs):
    channels, rows, cells = tracer.shape
    lat_count = lax.axis_size("lat")
    lat, lon = lax.axis_index("lat"), lax.axis_index("lon")
    blocks = source.reshape(rows)

    smem = pl.BlockSpec(memory_space=pltpu.SMEM)
    vmem = pl.BlockSpec(memory_space=pltpu.VMEM)
    anyplace = pl.BlockSpec(memory_space=pl.ANY)
    field = jax.ShapeDtypeStruct(tracer.shape, F32)

    def call(kernel, out_shape, in_specs, out_specs, scratch, limit, flops, **more):
        return pl.pallas_call(
            kernel,
            out_shape=out_shape,
            in_specs=in_specs,
            out_specs=out_specs,
            scratch_shapes=scratch,
            compiler_params=pltpu.CompilerParams(vmem_limit_bytes=limit << 20),
            cost_estimate=pl.CostEstimate(
                flops=flops, bytes_accessed=1 << 20, transcendentals=0
            ),
            **more,
        )

    def moved(values, target):
        pairs = []
        for a in range(lat_count):
            for b in range(NBLK):
                to = target(a, b)
                if 0 <= to[0] < lat_count:
                    pairs.append((a * NBLK + b, to[0] * NBLK + to[1] % NBLK))
        return lax.ppermute(values, ("lat", "lon"), pairs)

    dma = pltpu.SemaphoreType.DMA
    with jax.named_scope("lon_neighbours"):
        west = moved(tracer, lambda a, b: (a, b + 1))
        east = moved(tracer, lambda a, b: (a, b - 1))

    with jax.named_scope("pack_polar_band"):
        packed = call(
            pack_kernel,
            jax.ShapeDtypeStruct((NBLK, 4, PROWS, BLK), F32),
            [anyplace] * 4,
            anyplace,
            [
                pltpu.VMEM((1, rows), jnp.int32),
                pltpu.VMEM((channels, PROWS, BLK), F32),
                pltpu.VMEM((PROWS, BLK), jnp.int32),
                pltpu.VMEM((NBLK, 2, PROWS, BLK), F32),
                dma((6,)),
            ],
            60,
            1_000_000,
        )(source.reshape(1, rows), tracer, offset, fraction)

    def filter_band():
        band = lax.all_to_all(packed, "lon", 0, 0)
        tables = fourier_tables()
        damping = jax.ShapeDtypeStruct((HALF * PROWS, BLK), F32)
        held = [jax.ShapeDtypeStruct(table.shape, table.dtype) for table in tables]
        prepared = call(
            prepare_kernel,
            (damping, *held),
            [smem] + [vmem] * 4,
            (vmem,) * 5,
            [],
            16,
            1_000_000_000,
        )(cutoffs, *tables)
        return call(
            polar_kernel,
            jax.ShapeDtypeStruct((NBLK, 2, PROWS, BLK), F32),
            [vmem] * 6,
            vmem,
            [],
            16,
            400_000_000,
        )(band, *prepared)

    with jax.named_scope("polar_rows"):
        filtered = lax.cond(
            (lat == 0) | (lat == lat_count - 1),
            filter_band,
            lambda: jnp.zeros((NBLK, 2, PROWS, BLK), F32),
        )
        polar = lax.all_to_all(
            filtered, ("lat", "lon"), 0, 0, axis_index_groups=return_groups(lat_count)
        ).reshape(channels, PROWS, BLK)

    with jax.named_scope("borders"):
        border = jax.ShapeDtypeStruct((3, HL, channels, cells), F32)
        to_other = call(border_kernel, border, [vmem] * 3, vmem, [], 16, 1_000_000)(
            west, tracer, east
        )
        other = moved(to_other, lambda a, b: (a + (1 if a % 2 else -1), b))
        to_pair = call(border_kernel, border, [vmem] * 3 + [anyplace], vmem, [], 16, 1_000_000)(
            west, tracer, east, other
        )
        pair = moved(to_pair, lambda a, b: (a + (-1 if a % 2 else 1), b))

    with jax.named_scope("other_rows"):
        row = blocks // NBLK - lat * rows
        column = jnp.clip(jnp.mod(blocks % NBLK - lon + 1, NBLK), 0, 2)
        place = jnp.stack([column, row])
        done = call(
            rows_kernel,
            field,
            [smem] + [vmem] * 7,
            vmem,
            [pltpu.VMEM((4, rows, BLK), F32)],
            16,
            3_000_000_000,
        )(place, offset, fraction, east, tracer, west, other, pair)

    with jax.named_scope("merge"):
        return call(
            merge_kernel,
            field,
            [anyplace, anyplace],
            anyplace,
            [dma],
            4,
            1_000_000,
            input_output_aliases={0: 0},
        )(done, polar)


def solution(mesh):
    placed = (P(None, "lat", "lon"), P("lat", "lon"), P("lat", "lon"), P("lat", "lon"), P())
    return jax.shard_map(
        body, mesh=mesh, in_specs=placed, out_specs=P(None, "lat", "lon"), check_vma=False
    )
```

```python
import math

import jax
import jax.numpy as jnp
import ml_dtypes
import numpy as np
from jax import lax
from jax.experimental import pallas as pl
from jax.experimental.pallas import tpu as pltpu
from jax.sharding import PartitionSpec as P

NLON = 2048
BLK = 128
NBLK = NLON // BLK
HL = 2
HALF = NBLK // 2 + 1
PROWS = 8
FIRST, FIRST_BACK = 5, 11
SHIFT = (FIRST - FIRST_BACK) % (2048 // 128)
F32 = jnp.float32
BF16 = jnp.bfloat16


def cubic_weights(position):
    return (
        -position * (position - 1.0) * (position - 2.0) / 6.0,
        (position + 1.0) * (position - 1.0) * (position - 2.0) / 2.0,
        -(position + 1.0) * position * (position - 2.0) / 2.0,
        (position + 1.0) * position * (position - 1.0) / 6.0,
    )


def cubic_limited(values, cells, weights):
    def at(shift):
        return jnp.take_along_axis(values, cells + shift, axis=1, mode="promise_in_bounds")

    before_one, at_anchor, after_one, after_two = at(-1), at(0), at(1), at(2)
    interpolated = (
        weights[0] * before_one
        + weights[1] * at_anchor
        + weights[2] * after_one
        + weights[3] * after_two
    )
    lowest_bound = jnp.minimum(at_anchor, after_one)
    upper_bound = jnp.maximum(at_anchor, after_one)
    return jnp.minimum(jnp.maximum(interpolated, lowest_bound), upper_bound)


def three_products(table, axis):
    high = table.astype(ml_dtypes.bfloat16)
    low = (table - high.astype(np.float64)).astype(ml_dtypes.bfloat16)
    return np.concatenate([high, high, low], axis)


def fourier_tables():
    b, k1 = np.arange(NBLK), np.arange(HALF)
    angles = 2.0 * math.pi * np.outer(k1, b) / NBLK
    rows = np.eye(PROWS)
    blocks = np.concatenate([np.kron(np.cos(angles), rows), -np.kron(np.sin(angles), rows)], 0)
    twice = np.where((k1 == 0) | (k1 == NBLK // 2), 1.0, 2.0)
    back = blocks.T * np.tile(np.repeat(twice, PROWS), 2)[None, :]
    i = np.arange(BLK)
    angles = 2.0 * math.pi * (np.outer(i, i) % BLK) / BLK
    cosine, sine = np.cos(angles), np.sin(angles)
    cells = np.block([[cosine, -sine], [sine, cosine]])
    angles = 2.0 * math.pi * np.repeat(np.outer(k1, i), PROWS, 0) / NLON
    turn = np.stack([np.cos(angles), -np.sin(angles)]).astype(np.float32)
    return three_products(blocks, 1), three_products(back, 1), three_products(cells, 0), turn


def dot(left, right):
    return jnp.dot(left, right, preferred_element_type=F32)


def pieces(values, axis):
    high = values.astype(BF16)
    low = (values - high.astype(F32)).astype(BF16)
    return jnp.concatenate([high, low, high], axis)


def pack_kernel(source, tracer, offset, fraction, out, block, slab, cells, aux, sems):
    channels, rows = tracer.shape[0], tracer.shape[1]
    first = jnp.where(lax.axis_index("lat") == 0, 0, rows - PROWS)
    own = pl.ds(pl.multiple_of(first, PROWS), PROWS)
    copies = [
        pltpu.make_async_copy(source, block, sems.at[0]),
        pltpu.make_async_copy(offset.at[own, :], cells, sems.at[1]),
        pltpu.make_async_copy(fraction.at[own, :], aux.at[0, 1], sems.at[2]),
        pltpu.make_async_copy(tracer.at[:, own, :], slab, sems.at[3]),
    ]
    for copy in copies:
        copy.start()
    for copy in copies[:3]:
        copy.wait()
    spread = jnp.broadcast_to(block[...], (PROWS, rows))
    row = first + lax.broadcasted_iota(jnp.int32, (PROWS, rows), 0)
    mine = row == lax.broadcasted_iota(jnp.int32, (PROWS, rows), 1)
    source_block = jnp.sum(jnp.where(mine, spread, 0), axis=1, keepdims=True)
    anchor = (source_block * BLK + cells[...]).astype(F32)
    position = aux[0, 1]
    for n in range(NBLK):
        aux[n, 0] = anchor
        aux[n, 1] = position
    beside = pltpu.make_async_copy(aux, out.at[:, 2:4], sems.at[4])
    beside.start()
    copies[3].wait()
    share = slab.reshape(NBLK, channels // NBLK, PROWS, BLK)
    band = pltpu.make_async_copy(share, out.at[:, 0:2], sems.at[5])
    band.start()
    beside.wait()
    band.wait()


def prepare_kernel(cutoffs, *refs):
    tables, damping, held = refs[:4], refs[4], refs[5:]
    for table, copy in zip(tables, held):
        copy[...] = table[...]
    shape = (HALF * PROWS, BLK)
    row = lax.broadcasted_iota(jnp.int32, shape, 0)
    wave = (row >> 3) + NBLK * lax.broadcasted_iota(jnp.int32, shape, 1)
    wave = jnp.minimum(wave, NLON - wave)
    side = jnp.where(lax.axis_index("lat") == 0, 0, 1)
    kappa = jnp.zeros(shape, jnp.int32)
    for j in range(PROWS):
        kappa = jnp.where((row & (PROWS - 1)) == j, cutoffs[side, j], kappa)
    inside = (wave >= 1) & (wave < NLON // 2)
    ratio = kappa.astype(F32) / jnp.maximum(wave, 1).astype(F32)
    damping[...] = jnp.where(inside, jnp.maximum(1.0 - ratio, 0.0), 0.0) * (1.0 / NLON)


def polar_kernel(band, weights, blocks, back, cells, turn, out):
    count = NBLK * PROWS
    half = HALF * PROWS
    anchor = band[:, 2].reshape(count, BLK).astype(jnp.int32)
    place = (((anchor >> 7) - FIRST) & 15) * PROWS + ((anchor >> 11) & 7)
    lanes = lax.broadcasted_iota(jnp.int32, (count, BLK), 1)
    chosen = jnp.where(place == lanes, 1.0, 0.0).astype(BF16)
    own = jnp.concatenate([band[:, 0].reshape(count, BLK), band[:, 1].reshape(count, BLK)], 1)
    high = own.astype(BF16)
    rest = own - high.astype(F32)
    middle = rest.astype(BF16)
    low = (rest - middle.astype(F32)).astype(BF16)
    picked = dot(jnp.concatenate([chosen] * 3, 1), jnp.concatenate([high, middle, low], 0))
    cell = anchor & 127
    cubic = cubic_weights(band[:, 3].reshape(count, BLK))
    limited = [
        cubic_limited(picked[:, :BLK], cell, cubic),
        cubic_limited(picked[:, BLK:], cell, cubic),
    ]
    turn_r, turn_i = turn[0], turn[1]
    first = dot(blocks[...], pieces(jnp.concatenate(limited, 1), 0))
    parts = []
    for c in range(2):
        real, imag = first[:half, c * BLK : (c + 1) * BLK], first[half:, c * BLK : (c + 1) * BLK]
        parts.append(
            jnp.concatenate([real * turn_r - imag * turn_i, real * turn_i + imag * turn_r], 1)
        )
    spectrum = dot(pieces(jnp.concatenate(parts, 0), 1), cells[...])
    damping = jnp.concatenate([weights[...], weights[...]], 0)
    damped = jnp.concatenate([spectrum[:, BLK:] * damping, spectrum[:, :BLK] * damping], 1)
    second = dot(pieces(damped, 1), cells[...])
    reals, imags = [], []
    for c in range(2):
        imag, real = second[c * half : (c + 1) * half, :BLK], second[c * half : (c + 1) * half, BLK:]
        reals.append(real * turn_r + imag * turn_i)
        imags.append(imag * turn_r - real * turn_i)
    both = jnp.concatenate([jnp.concatenate(reals, 1), jnp.concatenate(imags, 1)], 0)
    removed = dot(back[...], pieces(both, 0))
    for c in range(2):
        kept = limited[c] - removed[:, c * BLK : (c + 1) * BLK]
        kept = kept.reshape(NBLK, PROWS, BLK)
        out[SHIFT:, c] = kept[: NBLK - SHIFT]
        if SHIFT:
            out[:SHIFT, c] = kept[NBLK - SHIFT :]


def column_rows(columns, first):
    channels, rows = columns[0].shape[0], columns[0].shape[1]
    flat = [column.reshape(channels * rows, BLK) for column in columns]
    return [part[pl.ds(first, channels, stride=rows), :] for part in flat]


def store_row(out, j, values):
    channels, rows = out.shape[0], out.shape[1]
    out.reshape(channels * rows, BLK)[pl.ds(j, channels, stride=rows), :] = values


def own_values(columns, column, row):
    west, own, east = column_rows(columns, jnp.clip(row, 0, columns[0].shape[1] - 1))
    return jnp.where(column == 0, west, jnp.where(column == 1, own, east))


def border_kernel(west, own, east, *refs):
    out = refs[-1]
    to_other = len(refs) == 1
    rows = own.shape[1]
    lower = (lax.axis_index("lat") % 2 == 1) == to_other
    first = jnp.where(lower, rows - HL, 0)
    for j in range(HL):
        for n, values in enumerate(column_rows((west, own, east), first + j)):
            out[n, j] = values


def row_values(columns, column, row, beyond, halo):
    beyond = jnp.clip(beyond, 0, HL - 1)
    outside = (row < 0) | (row >= columns[0].shape[1])
    return jnp.where(outside, halo(column, beyond), own_values(columns, column, row))


def rows_kernel(place, offset, fraction, east, own, west, other, pair, out, cubic):
    first_of_pair = lax.axis_index("lat") % 2 == 0
    channels, rows = own.shape[0], own.shape[1]
    columns = (west, own, east)
    for n, weight in enumerate(cubic_weights(fraction[...])):
        cubic[n] = weight

    def north(column, row):
        return jnp.where(first_of_pair, other[column, row], pair[column, row])

    def south(column, row):
        return jnp.where(first_of_pair, pair[column, row], other[column, row])

    for j in range(rows):
        column, row = place[0, j], place[1, j]
        if j < HL:
            values = row_values(columns, column, row, row + HL, north)
        elif j < rows - HL:
            values = own_values(columns, column, row)
        else:
            values = row_values(columns, column, row, row - rows, south)
        cells = jnp.broadcast_to(offset[j : j + 1, :], (channels, BLK))
        weights = [cubic[n, j : j + 1, :] for n in range(4)]
        store_row(out, j, cubic_limited(values, cells, weights))


def merge_kernel(rows_done, polar, out, sems):
    lat = lax.axis_index("lat")
    last = lax.axis_size("lat") - 1
    channels = out.shape[0]
    split = SHIFT * (channels // NBLK)

    @pl.when((lat == 0) | (lat == last))
    def _():
        rows = pl.ds(pl.multiple_of(jnp.where(lat == 0, 0, out.shape[1] - PROWS), PROWS), PROWS)
        copies = []
        for n, (here, there, count) in enumerate(
            ((split, 0, channels - split), (0, channels - split, split))
        ):
            if count:
                part = out.at[pl.ds(there, count), rows, :]
                copies.append(
                    pltpu.make_async_copy(polar.at[pl.ds(here, count)], part, sems.at[n])
                )
        for copy in copies:
            copy.start()
        for copy in copies:
            copy.wait()


def around_circle(band, first):
    return [band * NBLK + (b + first) % NBLK for b in range(NBLK)]


def return_groups(lat_count):
    last = lat_count - 1
    planes = [b + half for b in range(NBLK // 2) for half in (0, NBLK // 2)]
    others = [a * NBLK + b for b in planes for a in range(1, last)]
    return [around_circle(0, FIRST_BACK), around_circle(last, FIRST_BACK)] + [others[n : n + NBLK] for n in range(0, len(others), NBLK)]


def body(tracer, source, offset, fraction, cutoffs):
    channels, rows, cells = tracer.shape
    lat_count = lax.axis_size("lat")
    lat, lon = lax.axis_index("lat"), lax.axis_index("lon")
    blocks = source.reshape(rows)

    smem = pl.BlockSpec(memory_space=pltpu.SMEM)
    vmem = pl.BlockSpec(memory_space=pltpu.VMEM)
    anyplace = pl.BlockSpec(memory_space=pl.ANY)
    field = jax.ShapeDtypeStruct(tracer.shape, F32)

    def call(kernel, out_shape, in_specs, out_specs, scratch, limit, flops, **more):
        return pl.pallas_call(
            kernel,
            out_shape=out_shape,
            in_specs=in_specs,
            out_specs=out_specs,
            scratch_shapes=scratch,
            compiler_params=pltpu.CompilerParams(vmem_limit_bytes=limit << 20),
            cost_estimate=pl.CostEstimate(
                flops=flops, bytes_accessed=1 << 20, transcendentals=0
            ),
            **more,
        )

    def moved(values, target):
        pairs = []
        for a in range(lat_count):
            for b in range(NBLK):
                to = target(a, b)
                if 0 <= to[0] < lat_count:
                    pairs.append((a * NBLK + b, to[0] * NBLK + to[1] % NBLK))
        return lax.ppermute(values, ("lat", "lon"), pairs)

    dma = pltpu.SemaphoreType.DMA
    with jax.named_scope("lon_neighbours"):
        west = moved(tracer, lambda a, b: (a, b + 1))
        east = moved(tracer, lambda a, b: (a, b - 1))

    with jax.named_scope("pack_polar_band"):
        packed = call(
            pack_kernel,
            jax.ShapeDtypeStruct((NBLK, 4, PROWS, BLK), F32),
            [anyplace] * 4,
            anyplace,
            [
                pltpu.VMEM((1, rows), jnp.int32),
                pltpu.VMEM((channels, PROWS, BLK), F32),
                pltpu.VMEM((PROWS, BLK), jnp.int32),
                pltpu.VMEM((NBLK, 2, PROWS, BLK), F32),
                dma((6,)),
            ],
            60,
            1_000_000,
        )(source.reshape(1, rows), tracer, offset, fraction)

    def filter_band():
        groups = [around_circle(a, FIRST) for a in range(lat_count)]
        band = lax.all_to_all(packed, ("lat", "lon"), 0, 0, axis_index_groups=groups)
        tables = fourier_tables()
        damping = jax.ShapeDtypeStruct((HALF * PROWS, BLK), F32)
        held = [jax.ShapeDtypeStruct(table.shape, table.dtype) for table in tables]
        prepared = call(
            prepare_kernel,
            (damping, *held),
            [smem] + [vmem] * 4,
            (vmem,) * 5,
            [],
            16,
            1_000_000_000,
        )(cutoffs, *tables)
        return call(
            polar_kernel,
            jax.ShapeDtypeStruct((NBLK, 2, PROWS, BLK), F32),
            [vmem] * 6,
            vmem,
            [],
            16,
            400_000_000,
        )(band, *prepared)

    with jax.named_scope("polar_rows"):
        filtered = lax.cond(
            (lat == 0) | (lat == lat_count - 1),
            filter_band,
            lambda: jnp.zeros((NBLK, 2, PROWS, BLK), F32),
        )
        polar = lax.all_to_all(
            filtered, ("lat", "lon"), 0, 0, axis_index_groups=return_groups(lat_count)
        ).reshape(channels, PROWS, BLK)

    with jax.named_scope("borders"):
        border = jax.ShapeDtypeStruct((3, HL, channels, cells), F32)
        to_other = call(border_kernel, border, [vmem] * 3, vmem, [], 16, 1_000_000)(
            west, tracer, east
        )
        other = moved(to_other, lambda a, b: (a + (1 if a % 2 else -1), b))
        to_pair = call(border_kernel, border, [vmem] * 3 + [anyplace], vmem, [], 16, 1_000_000)(
            west, tracer, east, other
        )
        pair = moved(to_pair, lambda a, b: (a + (-1 if a % 2 else 1), b))

    with jax.named_scope("other_rows"):
        row = blocks // NBLK - lat * rows
        column = jnp.clip(jnp.mod(blocks % NBLK - lon + 1, NBLK), 0, 2)
        place = jnp.stack([column, row])
        done = call(
            rows_kernel,
            field,
            [smem] + [vmem] * 7,
            vmem,
            [pltpu.VMEM((4, rows, BLK), F32)],
            16,
            3_000_000_000,
        )(place, offset, fraction, east, tracer, west, other, pair)

    with jax.named_scope("merge"):
        return call(
            merge_kernel,
            field,
            [anyplace, anyplace],
            anyplace,
            [dma((2,))],
            4,
            1_000_000,
            input_output_aliases={0: 0},
        )(done, polar)


def solution(mesh):
    placed = (P(None, "lat", "lon"), P("lat", "lon"), P("lat", "lon"), P("lat", "lon"), P())
    return jax.shard_map(
        body, mesh=mesh, in_specs=placed, out_specs=P(None, "lat", "lon"), check_vma=False
    )
```

```python
import math

import jax
import jax.numpy as jnp
import ml_dtypes
import numpy as np
from jax import lax
from jax.experimental import pallas as pl
from jax.experimental.pallas import tpu as pltpu
from jax.sharding import PartitionSpec as P

NLON = 2048
BLK = 128
NBLK = NLON // BLK
HL = 2
HALF = NBLK // 2 + 1
PROWS = 8
FIRST, FIRST_BACK = 5, 11
SHIFT = (FIRST - FIRST_BACK) % (2048 // 128)
F32 = jnp.float32
SIXTH = 1.0 / 6.0
BF16 = jnp.bfloat16


def cubic_weights(position):
    return (
        -position * (position - 1.0) * (position - 2.0) * SIXTH,
        (position + 1.0) * (position - 1.0) * (position - 2.0) * 0.5,
        -(position + 1.0) * position * (position - 2.0) * 0.5,
        (position + 1.0) * position * (position - 1.0) * SIXTH,
    )


def cubic_limited(values, cells, weights):
    def at(shift):
        return jnp.take_along_axis(values, cells + shift, axis=1, mode="promise_in_bounds")

    before_one, at_anchor, after_one, after_two = at(-1), at(0), at(1), at(2)
    interpolated = (
        weights[0] * before_one
        + weights[1] * at_anchor
        + weights[2] * after_one
        + weights[3] * after_two
    )
    lowest_bound = jnp.minimum(at_anchor, after_one)
    upper_bound = jnp.maximum(at_anchor, after_one)
    return jnp.minimum(jnp.maximum(interpolated, lowest_bound), upper_bound)


def three_products(table, axis):
    high = table.astype(ml_dtypes.bfloat16)
    low = (table - high.astype(np.float64)).astype(ml_dtypes.bfloat16)
    return np.concatenate([high, high, low], axis)


def fourier_tables():
    b, k1 = np.arange(NBLK), np.arange(HALF)
    angles = 2.0 * math.pi * np.outer(k1, b) / NBLK
    rows = np.eye(PROWS)
    blocks = np.concatenate([np.kron(np.cos(angles), rows), -np.kron(np.sin(angles), rows)], 0)
    twice = np.where((k1 == 0) | (k1 == NBLK // 2), 1.0, 2.0)
    back = blocks.T * np.tile(np.repeat(twice, PROWS), 2)[None, :]
    i = np.arange(BLK)
    angles = 2.0 * math.pi * (np.outer(i, i) % BLK) / BLK
    cosine, sine = np.cos(angles), np.sin(angles)
    cells = np.block([[cosine, -sine], [sine, cosine]])
    angles = 2.0 * math.pi * np.repeat(np.outer(k1, i), PROWS, 0) / NLON
    turn = np.stack([np.cos(angles), -np.sin(angles)]).astype(np.float32)
    return three_products(blocks, 1), three_products(back, 1), three_products(cells, 0), turn


def dot(left, right):
    return jnp.dot(left, right, preferred_element_type=F32)


def pieces(values, axis):
    high = values.astype(BF16)
    low = (values - high.astype(F32)).astype(BF16)
    return jnp.concatenate([high, low, high], axis)


def pack_kernel(source, tracer, offset, fraction, out, block, slab, cells, aux, sems):
    channels, rows = tracer.shape[0], tracer.shape[1]
    first = jnp.where(lax.axis_index("lat") == 0, 0, rows - PROWS)
    own = pl.ds(pl.multiple_of(first, PROWS), PROWS)
    copies = [
        pltpu.make_async_copy(source, block, sems.at[0]),
        pltpu.make_async_copy(offset.at[own, :], cells, sems.at[1]),
        pltpu.make_async_copy(fraction.at[own, :], aux.at[0, 1], sems.at[2]),
        pltpu.make_async_copy(tracer.at[:, own, :], slab, sems.at[3]),
    ]
    for copy in copies:
        copy.start()
    for copy in copies[:3]:
        copy.wait()
    spread = jnp.broadcast_to(block[...], (PROWS, rows))
    row = first + lax.broadcasted_iota(jnp.int32, (PROWS, rows), 0)
    mine = row == lax.broadcasted_iota(jnp.int32, (PROWS, rows), 1)
    source_block = jnp.sum(jnp.where(mine, spread, 0), axis=1, keepdims=True)
    anchor = (source_block * BLK + cells[...]).astype(F32)
    position = aux[0, 1]
    for n in range(NBLK):
        aux[n, 0] = anchor
        aux[n, 1] = position
    beside = pltpu.make_async_copy(aux, out.at[:, 2:4], sems.at[4])
    beside.start()
    copies[3].wait()
    share = slab.reshape(NBLK, channels // NBLK, PROWS, BLK)
    band = pltpu.make_async_copy(share, out.at[:, 0:2], sems.at[5])
    band.start()
    beside.wait()
    band.wait()


def prepare_kernel(cutoffs, *refs):
    tables, damping, held = refs[:4], refs[4], refs[5:]
    for table, copy in zip(tables, held):
        copy[...] = table[...]
    shape = (HALF * PROWS, BLK)
    row = lax.broadcasted_iota(jnp.int32, shape, 0)
    wave = (row >> 3) + NBLK * lax.broadcasted_iota(jnp.int32, shape, 1)
    wave = jnp.minimum(wave, NLON - wave)
    side = jnp.where(lax.axis_index("lat") == 0, 0, 1)
    kappa = jnp.zeros(shape, jnp.int32)
    for j in range(PROWS):
        kappa = jnp.where((row & (PROWS - 1)) == j, cutoffs[side, j], kappa)
    inside = (wave >= 1) & (wave < NLON // 2)
    ratio = kappa.astype(F32) / jnp.maximum(wave, 1).astype(F32)
    damping[...] = jnp.where(inside, jnp.maximum(1.0 - ratio, 0.0), 0.0) * (1.0 / NLON)


def polar_kernel(band, weights, blocks, back, cells, turn, out):
    count = NBLK * PROWS
    half = HALF * PROWS
    anchor = band[:, 2].reshape(count, BLK).astype(jnp.int32)
    place = (((anchor >> 7) - FIRST) & 15) * PROWS + ((anchor >> 11) & 7)
    lanes = lax.broadcasted_iota(jnp.int32, (count, BLK), 1)
    chosen = jnp.where(place == lanes, 1.0, 0.0).astype(BF16)
    own = jnp.concatenate([band[:, 0].reshape(count, BLK), band[:, 1].reshape(count, BLK)], 1)
    high = own.astype(BF16)
    rest = own - high.astype(F32)
    middle = rest.astype(BF16)
    low = (rest - middle.astype(F32)).astype(BF16)
    picked = dot(jnp.concatenate([chosen] * 3, 1), jnp.concatenate([high, middle, low], 0))
    cell = anchor & 127
    cubic = cubic_weights(band[:, 3].reshape(count, BLK))
    limited = [
        cubic_limited(picked[:, :BLK], cell, cubic),
        cubic_limited(picked[:, BLK:], cell, cubic),
    ]
    turn_r, turn_i = turn[0], turn[1]
    first = dot(blocks[...], pieces(jnp.concatenate(limited, 1), 0))
    parts = []
    for c in range(2):
        real, imag = first[:half, c * BLK : (c + 1) * BLK], first[half:, c * BLK : (c + 1) * BLK]
        parts.append(
            jnp.concatenate([real * turn_r - imag * turn_i, real * turn_i + imag * turn_r], 1)
        )
    spectrum = dot(pieces(jnp.concatenate(parts, 0), 1), cells[...])
    damping = jnp.concatenate([weights[...], weights[...]], 0)
    damped = jnp.concatenate([spectrum[:, BLK:] * damping, spectrum[:, :BLK] * damping], 1)
    second = dot(pieces(damped, 1), cells[...])
    reals, imags = [], []
    for c in range(2):
        imag, real = second[c * half : (c + 1) * half, :BLK], second[c * half : (c + 1) * half, BLK:]
        reals.append(real * turn_r + imag * turn_i)
        imags.append(imag * turn_r - real * turn_i)
    both = jnp.concatenate([jnp.concatenate(reals, 1), jnp.concatenate(imags, 1)], 0)
    removed = dot(back[...], pieces(both, 0))
    for c in range(2):
        kept = limited[c] - removed[:, c * BLK : (c + 1) * BLK]
        kept = kept.reshape(NBLK, PROWS, BLK)
        out[SHIFT:, c] = kept[: NBLK - SHIFT]
        if SHIFT:
            out[:SHIFT, c] = kept[NBLK - SHIFT :]


def column_rows(columns, first):
    channels, rows = columns[0].shape[0], columns[0].shape[1]
    flat = [column.reshape(channels * rows, BLK) for column in columns]
    return [part[pl.ds(first, channels, stride=rows), :] for part in flat]


def store_row(out, j, values):
    channels, rows = out.shape[0], out.shape[1]
    out.reshape(channels * rows, BLK)[pl.ds(j, channels, stride=rows), :] = values


def own_values(columns, column, row):
    west, own, east = column_rows(columns, jnp.clip(row, 0, columns[0].shape[1] - 1))
    return jnp.where(column == 0, west, jnp.where(column == 1, own, east))


def border_kernel(west, own, east, *refs):
    out = refs[-1]
    to_other = len(refs) == 1
    rows = own.shape[1]
    lower = (lax.axis_index("lat") % 2 == 1) == to_other
    first = jnp.where(lower, rows - HL, 0)
    for j in range(HL):
        for n, values in enumerate(column_rows((west, own, east), first + j)):
            out[n, j] = values


def row_values(columns, column, row, beyond, halo):
    beyond = jnp.clip(beyond, 0, HL - 1)
    outside = (row < 0) | (row >= columns[0].shape[1])
    return jnp.where(outside, halo(column, beyond), own_values(columns, column, row))


def rows_kernel(place, offset, fraction, east, own, west, other, pair, out, cubic):
    first_of_pair = lax.axis_index("lat") % 2 == 0
    channels, rows = own.shape[0], own.shape[1]
    columns = (west, own, east)
    for n, weight in enumerate(cubic_weights(fraction[...])):
        cubic[n] = weight

    def north(column, row):
        return jnp.where(first_of_pair, other[column, row], pair[column, row])

    def south(column, row):
        return jnp.where(first_of_pair, pair[column, row], other[column, row])

    for j in range(rows):
        column, row = place[0, j], place[1, j]
        if j < HL:
            values = row_values(columns, column, row, row + HL, north)
        elif j < rows - HL:
            values = own_values(columns, column, row)
        else:
            values = row_values(columns, column, row, row - rows, south)
        cells = jnp.broadcast_to(offset[j : j + 1, :], (channels, BLK))
        weights = [cubic[n, j : j + 1, :] for n in range(4)]
        store_row(out, j, cubic_limited(values, cells, weights))


def merge_kernel(rows_done, polar, out, sems):
    lat = lax.axis_index("lat")
    last = lax.axis_size("lat") - 1
    channels = out.shape[0]
    split = SHIFT * (channels // NBLK)

    @pl.when((lat == 0) | (lat == last))
    def _():
        rows = pl.ds(pl.multiple_of(jnp.where(lat == 0, 0, out.shape[1] - PROWS), PROWS), PROWS)
        copies = []
        for n, (here, there, count) in enumerate(
            ((split, 0, channels - split), (0, channels - split, split))
        ):
            if count:
                part = out.at[pl.ds(there, count), rows, :]
                copies.append(
                    pltpu.make_async_copy(polar.at[pl.ds(here, count)], part, sems.at[n])
                )
        for copy in copies:
            copy.start()
        for copy in copies:
            copy.wait()


def around_circle(band, first):
    return [band * NBLK + (b + first) % NBLK for b in range(NBLK)]


def return_groups(lat_count):
    last = lat_count - 1
    planes = [b + half for b in range(NBLK // 2) for half in (0, NBLK // 2)]
    others = [a * NBLK + b for b in planes for a in range(1, last)]
    return [around_circle(0, FIRST_BACK), around_circle(last, FIRST_BACK)] + [others[n : n + NBLK] for n in range(0, len(others), NBLK)]


def body(tracer, source, offset, fraction, cutoffs):
    channels, rows, cells = tracer.shape
    lat_count = lax.axis_size("lat")
    lat, lon = lax.axis_index("lat"), lax.axis_index("lon")
    blocks = source.reshape(rows)

    smem = pl.BlockSpec(memory_space=pltpu.SMEM)
    vmem = pl.BlockSpec(memory_space=pltpu.VMEM)
    anyplace = pl.BlockSpec(memory_space=pl.ANY)
    field = jax.ShapeDtypeStruct(tracer.shape, F32)

    def call(kernel, out_shape, in_specs, out_specs, scratch, limit, flops, **more):
        return pl.pallas_call(
            kernel,
            out_shape=out_shape,
            in_specs=in_specs,
            out_specs=out_specs,
            scratch_shapes=scratch,
            compiler_params=pltpu.CompilerParams(vmem_limit_bytes=limit << 20),
            cost_estimate=pl.CostEstimate(
                flops=flops, bytes_accessed=1 << 20, transcendentals=0
            ),
            **more,
        )

    def moved(values, target):
        pairs = []
        for a in range(lat_count):
            for b in range(NBLK):
                to = target(a, b)
                if 0 <= to[0] < lat_count:
                    pairs.append((a * NBLK + b, to[0] * NBLK + to[1] % NBLK))
        return lax.ppermute(values, ("lat", "lon"), pairs)

    dma = pltpu.SemaphoreType.DMA
    with jax.named_scope("lon_neighbours"):
        west = moved(tracer, lambda a, b: (a, b + 1))
        east = moved(tracer, lambda a, b: (a, b - 1))

    with jax.named_scope("pack_polar_band"):
        packed = call(
            pack_kernel,
            jax.ShapeDtypeStruct((NBLK, 4, PROWS, BLK), F32),
            [anyplace] * 4,
            anyplace,
            [
                pltpu.VMEM((1, rows), jnp.int32),
                pltpu.VMEM((channels, PROWS, BLK), F32),
                pltpu.VMEM((PROWS, BLK), jnp.int32),
                pltpu.VMEM((NBLK, 2, PROWS, BLK), F32),
                dma((6,)),
            ],
            60,
            1_000_000,
        )(source.reshape(1, rows), tracer, offset, fraction)

    def filter_band():
        groups = [around_circle(a, FIRST) for a in range(lat_count)]
        band = lax.all_to_all(packed, ("lat", "lon"), 0, 0, axis_index_groups=groups)
        tables = fourier_tables()
        damping = jax.ShapeDtypeStruct((HALF * PROWS, BLK), F32)
        held = [jax.ShapeDtypeStruct(table.shape, table.dtype) for table in tables]
        prepared = call(
            prepare_kernel,
            (damping, *held),
            [smem] + [vmem] * 4,
            (vmem,) * 5,
            [],
            16,
            1_000_000_000,
        )(cutoffs, *tables)
        return call(
            polar_kernel,
            jax.ShapeDtypeStruct((NBLK, 2, PROWS, BLK), F32),
            [vmem] * 6,
            vmem,
            [],
            16,
            400_000_000,
        )(band, *prepared)

    with jax.named_scope("polar_rows"):
        filtered = lax.cond(
            (lat == 0) | (lat == lat_count - 1),
            filter_band,
            lambda: jnp.zeros((NBLK, 2, PROWS, BLK), F32),
        )
        polar = lax.all_to_all(
            filtered, ("lat", "lon"), 0, 0, axis_index_groups=return_groups(lat_count)
        ).reshape(channels, PROWS, BLK)

    with jax.named_scope("borders"):
        border = jax.ShapeDtypeStruct((3, HL, channels, cells), F32)
        to_other = call(border_kernel, border, [vmem] * 3, vmem, [], 16, 1_000_000)(
            west, tracer, east
        )
        other = moved(to_other, lambda a, b: (a + (1 if a % 2 else -1), b))
        to_pair = call(border_kernel, border, [vmem] * 3 + [anyplace], vmem, [], 16, 1_000_000)(
            west, tracer, east, other
        )
        pair = moved(to_pair, lambda a, b: (a + (-1 if a % 2 else 1), b))

    with jax.named_scope("other_rows"):
        row = blocks // NBLK - lat * rows
        column = jnp.clip(jnp.mod(blocks % NBLK - lon + 1, NBLK), 0, 2)
        place = jnp.stack([column, row])
        done = call(
            rows_kernel,
            field,
            [smem] + [vmem] * 7,
            vmem,
            [pltpu.VMEM((4, rows, BLK), F32)],
            16,
            3_000_000_000,
        )(place, offset, fraction, east, tracer, west, other, pair)

    with jax.named_scope("merge"):
        return call(
            merge_kernel,
            field,
            [anyplace, anyplace],
            anyplace,
            [dma((2,))],
            4,
            1_000_000,
            input_output_aliases={0: 0},
        )(done, polar)


def solution(mesh):
    placed = (P(None, "lat", "lon"), P("lat", "lon"), P("lat", "lon"), P("lat", "lon"), P())
    return jax.shard_map(
        body, mesh=mesh, in_specs=placed, out_specs=P(None, "lat", "lon"), check_vma=False
    )
```
